32 devices in a mesh: win: 2 (over y), tx: 4 (over z), ty: 4 (over x, core).
Axes of the slice: x: 2, y: 2, z: 4, core: 2. Of those that a mesh axis runs over, the one named last changes fastest.
Arguments:
- dual: float32 [2, 4, 4, 256, 512], P('win', None, None, 'ty', 'tx'), may hold values from -6 to 6
- obs_dual: float32 [2, 2, 256, 512], P('win', None, 'ty', 'tx'), may hold values from -6 to 6
- increment: float32 [2, 4, 4, 256, 512], P('win', None, None, 'ty', 'tx'), may hold values from -6 to 6
- trajectory: float32 [2, 3, 2, 4, 256, 512], P('win', None, None, None, 'ty', 'tx'), may hold values from -0.3 to 0.3
- diffusion: float32 [4, 4], replicated, may hold values from 0.01 to 0.045
- obs_weight: float32 [2, 4, 4], replicated, may hold values from -1.5 to 1.5
- model_var: float32 [2, 4, 4, 256, 512], P('win', None, None, 'ty', 'tx'), may hold values from 0.3 to 3
- obs_var: float32 [2, 2, 256, 512], P('win', None, 'ty', 'tx'), may hold values from 0.5 to 2
Outputs:
- next_dual: float32 [2, 4, 4, 256, 512], P('win', None, None, 'ty', 'tx')
- next_obs: float32 [2, 2, 256, 512], P('win', None, 'ty', 'tx')
- next_increment: float32 [2, 4, 4, 256, 512], P('win', None, None, 'ty', 'tx')
- coeffs: float32 [2], replicated
The draws below stay inside these ranges and needn't reach their ends.
All inputs are finite; a program needn't handle non-finite values.
Results may differ from the reference program's by a relative error of at most 0.00016.
Values sent between devices are 32-bit elements; how exact they have to be, the bound alone decides.
A program may use at most 128 MiB of HBM per device.

```python
import math
import jax
import jax.numpy as jnp
from jax import lax

F = 4
LEV = 4
STEPS = 3
NOBS = 2
W = 2
NLAT = 256
NLON = 512


def steps_of(stream_key, shape, pieces, least, high):
    gain, own = 1.0, jax.random.fold_in(stream_key, 6)
    for position, blocks in pieces:
        steps = jnp.exp(jax.random.uniform(jax.random.fold_in(own, position), (blocks,), jnp.float32, least / len(pieces), high / len(pieces)))
        gain = gain * jnp.repeat(steps, shape[position] // blocks).reshape([-1 if axis == position else 1 for axis in range(len(shape))])
    return gain


def normal_values(key, dims, spread, most, split=(), held_as=jnp.bfloat16):
    loudness = steps_of(key, dims, split, -0.22, 0.18) if split else 1.0
    values = jax.random.normal(key, dims, jnp.float32) * spread * loudness
    return jnp.minimum(jnp.maximum(values, -most), most).astype(held_as)


def setup_inputs(seed: int = 0) -> dict:
    key_list = jax.random.split(jax.random.key(seed), 9)
    dual = normal_values(key_list[0], (W, F, LEV, NLAT, NLON), 1.0, 6.0, ((0, 2), (3, 4), (4, 4)), jnp.float32)
    obs_dual = normal_values(key_list[1], (W, NOBS, NLAT, NLON), 1.0, 6.0, ((0, 2), (2, 4), (3, 4)), jnp.float32)
    increment = normal_values(key_list[2], (W, F, LEV, NLAT, NLON), 1.0, 6.0, ((0, 2), (3, 4), (4, 4)), jnp.float32)
    trajectory = jnp.clip(jax.random.uniform(key_list[3], (W, STEPS, 2, LEV, NLAT, NLON), jnp.float32, -0.3, 0.3) * steps_of(key_list[3], (W, STEPS, 2, LEV, NLAT, NLON), ((0, 2), (4, 4), (5, 4)), -0.4, 0.0), -0.3, 0.3)
    diffusion = jnp.clip(jnp.exp(jax.random.uniform(key_list[4], (F, LEV), jnp.float32, math.log(0.01), math.log(0.045))), 0.01, 0.045)
    obs_weight = normal_values(key_list[5], (NOBS, F, LEV), (F * LEV) ** -0.5, 1.5, (), jnp.float32)
    model_var = jnp.clip(jnp.exp(math.log(3.0) - 2.3025851 * jax.random.uniform(key_list[6], (W, F, LEV, NLAT, NLON), jnp.float32) ** steps_of(key_list[6], (W, F, LEV, NLAT, NLON), ((0, 2), (3, 4), (4, 4)), -0.2, 0.2)), 0.3, 3.0)
    obs_var = jnp.clip(jnp.exp(math.log(2.0) - 1.3862944 * jax.random.uniform(key_list[7], (W, NOBS, NLAT, NLON), jnp.float32) ** steps_of(key_list[7], (W, NOBS, NLAT, NLON), ((0, 2), (2, 4), (3, 4)), -0.2, 0.2)), 0.5, 2.0)
    return dict(dual=dual, obs_dual=obs_dual, increment=increment, trajectory=trajectory, diffusion=diffusion, obs_weight=obs_weight, model_var=model_var, obs_var=obs_var)


def neighbours(field):
    east = jnp.roll(field, -1, axis=3)
    west = jnp.roll(field, 1, axis=3)
    zero_row = jnp.zeros_like(field[:, :, :1, :])
    north = jnp.concatenate([field[:, :, 1:, :], zero_row], axis=2)
    south = jnp.concatenate([zero_row, field[:, :, :-1, :]], axis=2)
    return (east, west, north, south)

def forward_step(field, wind_lon, wind_lat, diffuse):
    pos_lon = jnp.maximum(wind_lon, 0.0)[None]
    neg_lon = jnp.minimum(wind_lon, 0.0)[None]
    pos_lat = jnp.maximum(wind_lat, 0.0)[None]
    neg_lat = jnp.minimum(wind_lat, 0.0)[None]
    east, west, north, south = neighbours(field)
    return field - pos_lon * (field - west) - neg_lon * (east - field) - pos_lat * (field - south) - neg_lat * (north - field) + diffuse * (east + west + north + south - 4.0 * field)

def adjoint_step(field, wind_lon, wind_lat, diffuse):
    pos_lon = jnp.maximum(wind_lon, 0.0)[None]
    neg_lon = jnp.minimum(wind_lon, 0.0)[None]
    pos_lat = jnp.maximum(wind_lat, 0.0)[None]
    neg_lat = jnp.minimum(wind_lat, 0.0)[None]
    east, west, north, south = neighbours(field)
    east_pos = jnp.roll(pos_lon * field, -1, axis=3)
    west_neg = jnp.roll(neg_lon * field, 1, axis=3)
    north_pos = neighbours(pos_lat * field)[2]
    south_neg = neighbours(neg_lat * field)[3]
    diagonal = 1.0 - pos_lon + neg_lon - pos_lat + neg_lat - 4.0 * diffuse
    return diagonal * field + east_pos - west_neg + north_pos - south_neg + diffuse * (east + west + north + south)

def reference(dual, obs_dual, increment, trajectory, diffusion, obs_weight, model_var, obs_var):
    diffuse = diffusion[:, :, None, None]
    later_dual = jnp.concatenate([dual[1:], jnp.zeros_like(dual[:1])], axis=0)

    def window(items):
        state, winds, multipliers, following = items
        moved = state
        for index in range(STEPS):
            moved = forward_step(moved, winds[index, 0], winds[index, 1], diffuse)
        obs_end = jnp.einsum('ofl,flab->oab', obs_weight, moved, precision=lax.Precision.HIGHEST)
        adjoint_field = jnp.einsum('ofl,oab->flab', obs_weight, multipliers, precision=lax.Precision.HIGHEST) - following
        for index in reversed(range(STEPS)):
            adjoint_field = adjoint_step(adjoint_field, winds[index, 0], winds[index, 1], diffuse)
        return (moved, obs_end, adjoint_field)
    moved, obs_end, back = lax.map(window, (increment, trajectory, obs_dual, later_dual))
    carried = jnp.concatenate([jnp.zeros_like(moved[:1]), moved[:-1]], axis=0)
    zl = model_var * dual + increment - carried
    zm = obs_var * obs_dual + obs_end
    zd = dual + back
    new_lam = jnp.cumsum(zd[::-1], axis=0)[::-1]
    new_obs = zm / obs_var
    new_state = jnp.cumsum(zl - model_var * new_lam, axis=0)
    inner = jnp.sum(new_lam * dual) + jnp.sum(new_obs * obs_dual) + jnp.sum(new_state * increment)
    square = jnp.sum(dual * dual) + jnp.sum(obs_dual * obs_dual) + jnp.sum(increment * increment)
    coeff = inner / square
    rest_lam = new_lam - coeff * dual
    rest_obs = new_obs - coeff * obs_dual
    rest_state = new_state - coeff * increment
    rest_sq = jnp.sum(rest_lam * rest_lam) + jnp.sum(rest_obs * rest_obs) + jnp.sum(rest_state * rest_state)
    count = dual.size * 2 + obs_dual.size
    scale = jnp.sqrt(rest_sq / count + 1e-06)
    return (rest_lam / scale, rest_obs / scale, rest_state / scale, jnp.stack([coeff, scale]))
```

```python
import functools
import jax
import jax.numpy as jnp
from jax import lax
from jax.experimental import pallas as pl
from jax.experimental.pallas import tpu as pltpu
from jax.sharding import PartitionSpec as P

MESH = pl.DeviceIdType.MESH
PAD = 8
EAST, WEST, NORTH, SOUTH = range(4)


def kernel(sizes, dual, obs, inc, traj, mv, ov, diff, wgt,
           o_lam, o_obs, o_inc, o_co,
           fld, grd, back, foll, plin, pls, pxs, gin, gout, oend, sbuf, rbuf, red,
           h_send, h_recv, w_send, w_recv, r_send, r_recv):
    nwin, ntx, nty, steps, nf, nlev, rows, nobs, count = sizes
    groups = rows // 8
    win, tx, ty = lax.axis_index("win"), lax.axis_index("tx"), lax.axis_index("ty")
    has_prev, has_next = win > 0, win < nwin - 1
    right, left = lax.rem(tx + 1, ntx), lax.rem(tx + ntx - 1, ntx)
    lane = lax.broadcasted_iota(jnp.int32, (8, 128), 1)
    axes = (("ty", nty, ty), ("tx", ntx, tx), ("win", nwin, win))

    barrier = pltpu.get_barrier_semaphore()
    for name, n, me in axes:
        for j in range(1, n):
            pl.semaphore_signal(barrier, inc=1, device_id={name: lax.rem(me + j, n)}, device_id_type=MESH)

    @pl.when(ty == 0)
    def _():
        rbuf[:, :, :, SOUTH] = jnp.zeros((2, steps, nlev, 8, 128), jnp.float32)

    @pl.when(ty == nty - 1)
    def _():
        rbuf[:, :, :, NORTH] = jnp.zeros((2, steps, nlev, 8, 128), jnp.float32)

    @pl.when(win == nwin - 1)
    def _():
        foll[...] = jnp.zeros(foll.shape, jnp.float32)
        plin[...] = jnp.zeros(plin.shape, jnp.float32)

    pl.semaphore_wait(barrier, (nty - 1) + (ntx - 1) + (nwin - 1))

    def halo(kind, s, c, side):
        to = ({"tx": left}, {"tx": right}, {"ty": ty - 1}, {"ty": ty + 1})[side]
        return pltpu.make_async_remote_copy(
            src_ref=sbuf.at[kind, s, c, side], dst_ref=rbuf.at[kind, s, c, side],
            send_sem=h_send.at[kind, s, c, side], recv_sem=h_recv.at[kind, s, c, side],
            device_id=to, device_id_type=MESH)

    def sides(kind, s, c, act_send, act_recv):
        for side in range(4):
            copy = halo(kind, s, c, side)
            if side in (EAST, WEST):
                if act_send:
                    act_send(copy)
                if act_recv:
                    act_recv(copy)
                continue
            sends = ty > 0 if side == NORTH else ty < nty - 1
            gets = ty < nty - 1 if side == NORTH else ty > 0
            if act_send:
                pl.when(sends)(lambda copy=copy: act_send(copy))
            if act_recv:
                pl.when(gets)(lambda copy=copy: act_recv(copy))

    def start_halo(kind, s, c):
        sides(kind, s, c, lambda d: d.start(), None)

    def wait_halo(kind, s, c):
        sides(kind, s, c, None, lambda d: d.wait_recv())

    def wcopy(what, c):
        src, dst, to = (
            (dual.at[0, :, c], foll.at[c], win - 1),
            (pls.at[c], plin.at[c], win - 1),
            (gout.at[c], gin.at[c], win + 1),
        )[what]
        return pltpu.make_async_remote_copy(
            src_ref=src, dst_ref=dst, send_sem=w_send.at[what, c], recv_sem=w_recv.at[what, c],
            device_id={"win": to}, device_id_type=MESH)

    @pl.when(has_prev)
    def _():
        for c in range(nlev):
            wcopy(0, c).start()

    def loop(n, body):
        def step(i, carry):
            body(i)
            return carry
        lax.fori_loop(0, n, step, 0)

    def span(g):
        return pl.ds(8 * g, 8)

    def winds(s, c, g):
        a, b = traj[0, s, 0, c, span(g), :], traj[0, s, 1, c, span(g), :]
        pa, pb = jnp.maximum(a, 0.0), jnp.maximum(b, 0.0)
        ma, mb = pa - a, pb - b
        return pa, ma, pb, mb, 1.0 - ((pa + ma) + (pb + mb))

    def into(acc, value, column, k):
        return jnp.where(lane == k, pltpu.roll(value, (k - column) % 128, 1), acc)

    def outof(value, message, column, k):
        shift = 127 if column == 127 else 1
        return jnp.where(lane == column, pltpu.roll(message, (column - k) % 128, 1), pltpu.roll(value, shift, 1))

    zero_tile = jnp.zeros((8, 128), jnp.float32)

    def forward_first(c):
        first, last = zero_tile, zero_tile
        for p in range(nf):
            for g in range(groups):
                value = inc[0, p, c, span(g), :]
                fld[0, c, p, pl.ds(PAD + 8 * g, 8), :] = value
                first = into(first, value, 0, p * groups + g)
                last = into(last, value, 127, p * groups + g)
            sbuf[0, 0, c, NORTH, p, :] = inc[0, p, c, 0, :]
            sbuf[0, 0, c, SOUTH, p, :] = inc[0, p, c, rows - 1, :]
        sbuf[0, 0, c, EAST] = first
        sbuf[0, 0, c, WEST] = last
        start_halo(0, 0, c)

    loop(nlev, forward_first)

    def forward(s, c):
        wait_halo(0, s, c)
        now, later = lax.rem(s, 2), lax.rem(s + 1, 2)
        for p in range(nf):
            fld[now, c, p, PAD - 1, :] = rbuf[0, s, c, SOUTH, p, :]
            fld[now, c, p, PAD + rows, :] = rbuf[0, s, c, NORTH, p, :]
        from_east, from_west = rbuf[0, s, c, EAST], rbuf[0, s, c, WEST]
        first, last = zero_tile, zero_tile
        after = jnp.minimum(s + 1, steps - 1)
        for g in range(groups):
            pa, ma, pb, mb, d = winds(s, c, g)
            for p in range(nf):
                k = diff[p, c]
                x = fld[now, c, p, pl.ds(PAD + 8 * g, 8), :]
                north = fld[now, c, p, pl.ds(PAD + 8 * g + 1, 8), :]
                south = fld[now, c, p, pl.ds(PAD + 8 * g - 1, 8), :]
                place = p * groups + g
                east = outof(x, from_east, 127, place)
                west = outof(x, from_west, 0, place)
                new = (d - 4.0 * k) * x + (pa + k) * west + (ma + k) * east + (pb + k) * south + (mb + k) * north
                fld[later, c, p, pl.ds(PAD + 8 * g, 8), :] = new
                first = into(first, new, 0, place)
                last = into(last, new, 127, place)

        @pl.when(s < steps - 1)
        def _():
            for p in range(nf):
                sbuf[0, after, c, NORTH, p, :] = fld[later, c, p, PAD, :]
                sbuf[0, after, c, SOUTH, p, :] = fld[later, c, p, PAD + rows - 1, :]
            sbuf[0, after, c, EAST] = first
            sbuf[0, after, c, WEST] = last
            start_halo(0, after, c)

    loop(steps, lambda s: loop(nlev, lambda c: forward(s, c)))
    moved = fld.at[steps % 2]

    def products(y, w, k, slot, c, p, g):
        pa, ma, pb, mb, d = w
        g_east, g_west = (pa + k) * y, (ma + k) * y
        here = pl.ds(PAD + 8 * g, 8)
        grd[slot, 0, c, p, here, :] = g_east
        grd[slot, 1, c, p, here, :] = g_west
        grd[slot, 2, c, p, here, :] = (pb + k) * y
        grd[slot, 3, c, p, here, :] = (mb + k) * y
        grd[slot, 4, c, p, here, :] = (d - 4.0 * k) * y
        return g_east, g_west

    def ship(t, slot, c, first, last):
        for p in range(nf):
            sbuf[1, t, c, NORTH, p, :] = grd[slot, 2, c, p, PAD, :]
            sbuf[1, t, c, SOUTH, p, :] = grd[slot, 3, c, p, PAD + rows - 1, :]
        sbuf[1, t, c, EAST] = first
        sbuf[1, t, c, WEST] = last
        start_halo(1, t, c)

    def adjoint_first(c):
        @pl.when(has_next)
        def _():
            wcopy(0, c).wait_recv()

        first, last = zero_tile, zero_tile
        for g in range(groups):
            w = winds(steps - 1, c, g)
            for p in range(nf):
                y = -foll[c, p, span(g), :]
                for o in range(nobs):
                    y = y + wgt[o, p, c] * obs[0, o, span(g), :]
                g_east, g_west = products(y, w, diff[p, c], 0, c, p, g)
                first = into(first, g_east, 0, p * groups + g)
                last = into(last, g_west, 127, p * groups + g)
        ship(0, 0, c, first, last)

    loop(nlev, adjoint_first)

    def gathered(t, slot, c, p, g, from_east, from_west):
        here = pl.ds(PAD + 8 * g, 8)
        place = p * groups + g
        east = outof(grd[slot, 0, c, p, here, :], from_east, 127, place)
        west = outof(grd[slot, 1, c, p, here, :], from_west, 0, place)
        north = grd[slot, 2, c, p, pl.ds(PAD + 8 * g + 1, 8), :]
        south = grd[slot, 3, c, p, pl.ds(PAD + 8 * g - 1, 8), :]
        return grd[slot, 4, c, p, here, :] + ((east + west) + (north + south))

    def receive(t, slot, c):
        wait_halo(1, t, c)
        for p in range(nf):
            grd[slot, 2, c, p, PAD + rows, :] = rbuf[1, t, c, NORTH, p, :]
            grd[slot, 3, c, p, PAD - 1, :] = rbuf[1, t, c, SOUTH, p, :]
        return rbuf[1, t, c, EAST], rbuf[1, t, c, WEST]

    def adjoint(t, c):
        slot, other = lax.rem(t, 2), lax.rem(t + 1, 2)
        from_east, from_west = receive(t, slot, c)
        first, last = zero_tile, zero_tile
        for g in range(groups):
            w = winds(steps - 2 - t, c, g)
            for p in range(nf):
                y = gathered(t, slot, c, p, g, from_east, from_west)
                g_east, g_west = products(y, w, diff[p, c], other, c, p, g)
                first = into(first, g_east, 0, p * groups + g)
                last = into(last, g_west, 127, p * groups + g)
        ship(t + 1, other, c, first, last)

    loop(steps - 1, lambda t: loop(nlev, lambda c: adjoint(t, c)))

    def adjoint_last(c):
        slot = (steps - 1) % 2
        from_east, from_west = receive(steps - 1, slot, c)
        for g in range(groups):
            for p in range(nf):
                back[c, p, span(g), :] = gathered(steps - 1, slot, c, p, g, from_east, from_west)

        @pl.when(win == nwin - 1)
        def _():
            pls[c] = dual[0, :, c] + back[c]
            if nwin > 1:
                wcopy(1, c).start()

    loop(nlev, adjoint_last)

    def fold(x):
        return jnp.sum(x.reshape(-1, 8, 128), axis=0)

    def observe(c, carry):
        return tuple(
            sum((wgt[o, p, c] * moved[c, p, pl.ds(PAD, rows), :] for p in range(nf)), carry[o])
            for o in range(nobs))

    ends = lax.fori_loop(0, nlev, observe, tuple(jnp.zeros((rows, 128), jnp.float32) for _ in range(nobs)))
    wv0, vv0 = zero_tile, zero_tile
    for o in range(nobs):
        v = obs[0, o]
        pm = (ov[0, o] * v + ends[o]) / ov[0, o]
        oend[o] = pm
        wv0 = wv0 + fold(pm * v)
        vv0 = vv0 + fold(v * v)

    def squares(c, acc):
        return acc + fold(dual[0, :, c] * dual[0, :, c]) + fold(inc[0, :, c] * inc[0, :, c])

    vv = lax.fori_loop(0, nlev, squares, vv0)

    def suffix(c, acc):
        @pl.when(has_next)
        def _():
            wcopy(1, c).wait_recv()
            pls[c] = dual[0, :, c] + back[c] + plin[c]

        @pl.when(has_next & has_prev)
        def _():
            wcopy(1, c).start()

        lam = dual[0, :, c]
        new = pls[c]
        base = mv[0, :, c] * (lam - new) + inc[0, :, c]
        pxs[c] = base

        @pl.when((win == 0) & has_next)
        def _():
            gout[c] = base - moved[c, :, pl.ds(PAD, rows), :]
            wcopy(2, c).start()

        return acc + fold(new * lam)

    wv = lax.fori_loop(0, nlev, suffix, wv0)

    def prefix(c, acc):
        @pl.when(has_prev)
        def _():
            wcopy(2, c).wait_recv()
            pxs[c] = pxs[c] + gin[c]

        @pl.when(has_prev & has_next)
        def _():
            gout[c] = pxs[c] - moved[c, :, pl.ds(PAD, rows), :]
            wcopy(2, c).start()

        return acc + fold(pxs[c] * inc[0, :, c])

    wv = lax.fori_loop(0, nlev, prefix, wv)

    def total(x):
        return jnp.broadcast_to(jnp.sum(jnp.sum(x, axis=0, keepdims=True), axis=1, keepdims=True), (1, 128))

    def ratio(a, b):
        return jnp.where(b > 0.0, a / jnp.where(b > 0.0, b, 1.0), 0.0)

    wv, vv = total(wv), total(vv)
    h = ratio(wv, vv)

    def residual(c, acc):
        a = pls[c] - h[None] * dual[0, :, c]
        b = pxs[c] - h[None] * inc[0, :, c]
        return acc + fold(a * a) + fold(b * b)

    uu = zero_tile
    for o in range(nobs):
        r = oend[o] - h * obs[0, o]
        uu = uu + fold(r * r)
    uu = total(lax.fori_loop(0, nlev, residual, uu))

    at = 0
    for index, (name, n, me) in enumerate(axes):
        mine = red.at[at + me]
        red[at + me, 0:1, :] = uu
        red[at + me, 1:2, :] = wv
        red[at + me, 2:3, :] = vv

        def swap(j, name=name, n=n, me=me, at=at):
            return pltpu.make_async_remote_copy(
                src_ref=red.at[at + me], dst_ref=red.at[at + me],
                send_sem=r_send.at[at + j], recv_sem=r_recv.at[at + j],
                device_id={name: lax.rem(me + j, n)}, device_id_type=MESH)

        for j in range(1, n):
            swap(j).start()
        for j in range(1, n):
            swap(j).wait_recv()
        parts = [tuple(red[at + i, q:q + 1, :] for q in range(3)) for i in range(n)]
        wv = functools.reduce(lambda a, b: a + b, [q[1] for q in parts])
        vv = functools.reduce(lambda a, b: a + b, [q[2] for q in parts])
        h = ratio(wv, vv)
        uu = functools.reduce(
            lambda a, b: a + b, [q[0] + (ratio(q[1], q[2]) - h) * (ratio(q[1], q[2]) - h) * q[2] for q in parts])
        for j in range(1, n):
            swap(j).wait_send()
        at += n

    h = wv / vv
    scale = jnp.sqrt(uu / count + 1e-06)
    inv = 1.0 / scale
    o_co[0] = jnp.sum(jnp.where(lane[0:1] == 0, h, 0.0))
    o_co[1] = jnp.sum(jnp.where(lane[0:1] == 0, scale, 0.0))

    def finish(c):
        o_lam[0, :, c] = (pls[c] - h[None] * dual[0, :, c]) * inv[None]
        o_inc[0, :, c] = (pxs[c] - h[None] * inc[0, :, c]) * inv[None]

    loop(nlev, finish)
    for o in range(nobs):
        o_obs[0, o] = (oend[o] - h * obs[0, o]) * inv

    def settle(kind, s, c):
        sides(kind, s, c, lambda d: d.wait_send(), None)

    for kind in range(2):
        loop(steps, lambda s, kind=kind: loop(nlev, lambda c: settle(kind, s, c)))

    def settle_windows(c):
        @pl.when(has_prev)
        def _():
            wcopy(0, c).wait_send()
            wcopy(1, c).wait_send()

        @pl.when(has_next)
        def _():
            wcopy(2, c).wait_send()

    loop(nlev, settle_windows)


def per_device(mesh, dual, obs_dual, increment, trajectory, diffusion, obs_weight, model_var, obs_var):
    nwin, ntx, nty = (mesh.shape[a] for a in ("win", "tx", "ty"))
    _, nf, nlev, rows, cols = dual.shape
    nobs, steps = obs_dual.shape[1], trajectory.shape[1]
    assert cols == 128 and rows % 8 == 0 and nf * rows // 8 <= 128 and nf <= 8
    count = (2 * nf * nlev + nobs) * rows * cols * nwin * ntx * nty
    sizes = (nwin, ntx, nty, steps, nf, nlev, rows, nobs, float(count))
    vmem, smem = pl.BlockSpec(memory_space=pltpu.VMEM), pl.BlockSpec(memory_space=pltpu.SMEM)
    chunks = pltpu.VMEM((nlev, nf, rows, cols), jnp.float32)
    messages = pltpu.VMEM((2, steps, nlev, 4, 8, cols), jnp.float32)
    n_red = nwin + ntx + nty
    return pl.pallas_call(
        functools.partial(kernel, sizes),
        out_shape=(
            jax.ShapeDtypeStruct(dual.shape, jnp.float32),
            jax.ShapeDtypeStruct(obs_dual.shape, jnp.float32),
            jax.ShapeDtypeStruct(increment.shape, jnp.float32),
            jax.ShapeDtypeStruct((2,), jnp.float32),
        ),
        in_specs=[vmem] * 6 + [smem] * 2,
        out_specs=(vmem, vmem, vmem, smem),
        scratch_shapes=[
            pltpu.VMEM((2, nlev, nf, rows + 2 * PAD, cols), jnp.float32),
            pltpu.VMEM((2, 5, nlev, nf, rows + 2 * PAD, cols), jnp.float32),
            chunks, chunks, chunks, chunks, chunks, chunks, chunks,
            pltpu.VMEM((nobs, rows, cols), jnp.float32),
            messages, messages,
            pltpu.VMEM((n_red, 8, cols), jnp.float32),
            pltpu.SemaphoreType.DMA((2, steps, nlev, 4)),
            pltpu.SemaphoreType.DMA((2, steps, nlev, 4)),
            pltpu.SemaphoreType.DMA((3, nlev)),
            pltpu.SemaphoreType.DMA((3, nlev)),
            pltpu.SemaphoreType.DMA((n_red,)),
            pltpu.SemaphoreType.DMA((n_red,)),
        ],
        compiler_params=pltpu.CompilerParams(
            collective_id=0, has_side_effects=True, vmem_limit_bytes=48 * 1024 * 1024),
    )(dual, obs_dual, increment, trajectory, model_var, obs_var, diffusion, obs_weight)


def solution(mesh):
    in_specs = (
        P("win", None, None, "ty", "tx"),
        P("win", None, "ty", "tx"),
        P("win", None, None, "ty", "tx"),
        P("win", None, None, None, "ty", "tx"),
        P(),
        P(),
        P("win", None, None, "ty", "tx"),
        P("win", None, "ty", "tx"),
    )
    out_specs = (
        P("win", None, None, "ty", "tx"),
        P("win", None, "ty", "tx"),
        P("win", None, None, "ty", "tx"),
        P(),
    )
    return jax.shard_map(
        functools.partial(per_device, mesh), mesh=mesh, in_specs=in_specs, out_specs=out_specs, check_vma=False
    )
```

```python
import functools
import jax
import jax.numpy as jnp
from jax import lax
from jax.experimental import pallas as pl
from jax.experimental.pallas import tpu as pltpu
from jax.sharding import PartitionSpec as P

MESH = pl.DeviceIdType.MESH
PAD = 8
EAST, WEST, NORTH, SOUTH = range(4)


def kernel(sizes, h_dual, h_obs, h_inc, h_traj, h_mv, h_ov, h_diff, h_wgt,
           o_lam, o_obs, o_inc, o_co,
           dual, obs, inc, traj, mv, ov, diff, wgt, i_sem,
           fld, grd, back, foll, plin, pls, pxs, gin, gout, oend, sbuf, rbuf, red,
           h_send, h_recv, w_send, w_recv, r_send, r_recv):
    nwin, ntx, nty, steps, nf, nlev, rows, nobs, count = sizes
    groups = rows // 8
    win, tx, ty = lax.axis_index("win"), lax.axis_index("tx"), lax.axis_index("ty")
    has_prev, has_next = win > 0, win < nwin - 1
    right, left = lax.rem(tx + 1, ntx), lax.rem(tx + ntx - 1, ntx)
    lane = lax.broadcasted_iota(jnp.int32, (8, 128), 1)
    axes = (("ty", nty, ty), ("tx", ntx, tx), ("win", nwin, win))

    brought = [
        pltpu.make_async_copy(src, dst, i_sem.at[i])
        for i, (src, dst) in enumerate((
            (h_inc, inc), (h_diff, diff), (h_traj, traj), (h_obs, obs),
            (h_wgt, wgt), (h_dual, dual), (h_mv, mv), (h_ov, ov)))
    ]
    for copy in brought:
        copy.start()

    barrier = pltpu.get_barrier_semaphore()
    for name, n, me in axes:
        for j in range(1, n):
            pl.semaphore_signal(barrier, inc=1, device_id={name: lax.rem(me + j, n)}, device_id_type=MESH)

    @pl.when(win == nwin - 1)
    def _():
        foll[...] = jnp.zeros(foll.shape, jnp.float32)
        plin[...] = jnp.zeros(plin.shape, jnp.float32)

    pl.semaphore_wait(barrier, (nty - 1) + (ntx - 1) + (nwin - 1))

    north_of, south_of = lax.rem(ty + 1, nty), lax.rem(ty + nty - 1, nty)
    to = ({"tx": left}, {"tx": right}, {"ty": south_of}, {"ty": north_of})

    def start_halo(kind, s, c):
        for side in range(4):
            pltpu.make_async_remote_copy(
                src_ref=sbuf.at[kind, s, c, side], dst_ref=rbuf.at[kind, s, c, side],
                send_sem=h_send.at[kind], recv_sem=h_recv.at[kind, s, c],
                device_id=to[side], device_id_type=MESH).start()

    def wait_halo(kind, s, c):
        pltpu.make_async_remote_copy(
            src_ref=sbuf.at[kind, s, c], dst_ref=rbuf.at[kind, s, c],
            send_sem=h_send.at[kind], recv_sem=h_recv.at[kind, s, c],
            device_id=to[0], device_id_type=MESH).wait_recv()

    def edge_rows(kind, s, c):
        north = jnp.where(ty == nty - 1, 0.0, rbuf[kind, s, c, NORTH])
        south = jnp.where(ty == 0, 0.0, rbuf[kind, s, c, SOUTH])
        return north, south

    def wcopy(what, c):
        src, dst, to = (
            (h_dual.at[0, :, c], foll.at[c], win - 1),
            (pls.at[c], plin.at[c], win - 1),
            (gout.at[c], gin.at[c], win + 1),
        )[what]
        return pltpu.make_async_remote_copy(
            src_ref=src, dst_ref=dst, send_sem=w_send.at[what, c], recv_sem=w_recv.at[what, c],
            device_id={"win": to}, device_id_type=MESH)

    @pl.when(has_prev)
    def _():
        for c in range(nlev):
            wcopy(0, c).start()

    def loop(n, body):
        def step(i, carry):
            body(i)
            return carry
        lax.fori_loop(0, n, step, 0)

    def span(g):
        return pl.ds(8 * g, 8)

    def winds(s, c, g):
        a, b = traj[0, s, 0, c, span(g), :], traj[0, s, 1, c, span(g), :]
        pa, pb = jnp.maximum(a, 0.0), jnp.maximum(b, 0.0)
        ma, mb = pa - a, pb - b
        return pa, ma, pb, mb, 1.0 - ((pa + ma) + (pb + mb))

    def into(acc, value, column, k):
        return jnp.where(lane == k, pltpu.roll(value, (k - column) % 128, 1), acc)

    def outof(value, message, column, k):
        shift = 127 if column == 127 else 1
        return jnp.where(lane == column, pltpu.roll(message, (column - k) % 128, 1), pltpu.roll(value, shift, 1))

    zero_tile = jnp.zeros((8, 128), jnp.float32)

    def forward_first(c):
        first, last = zero_tile, zero_tile
        for p in range(nf):
            for g in range(groups):
                value = inc[0, p, c, span(g), :]
                fld[0, c, p, pl.ds(PAD + 8 * g, 8), :] = value
                first = into(first, value, 0, p * groups + g)
                last = into(last, value, 127, p * groups + g)
            sbuf[0, 0, c, NORTH, p, :] = inc[0, p, c, 0, :]
            sbuf[0, 0, c, SOUTH, p, :] = inc[0, p, c, rows - 1, :]
        sbuf[0, 0, c, EAST] = first
        sbuf[0, 0, c, WEST] = last
        start_halo(0, 0, c)

    brought[0].wait()
    loop(nlev, forward_first)
    brought[1].wait()
    brought[2].wait()

    def forward(s, c):
        wait_halo(0, s, c)
        now, later = lax.rem(s, 2), lax.rem(s + 1, 2)
        north_row, south_row = edge_rows(0, s, c)
        for p in range(nf):
            fld[now, c, p, PAD - 1, :] = south_row[p]
            fld[now, c, p, PAD + rows, :] = north_row[p]
        from_east, from_west = rbuf[0, s, c, EAST], rbuf[0, s, c, WEST]
        first, last = zero_tile, zero_tile
        after = jnp.minimum(s + 1, steps - 1)
        fresh = []
        for g in range(groups):
            pa, ma, pb, mb, d = winds(s, c, g)
            for p in range(nf):
                k = diff[p, c]
                x = fld[now, c, p, pl.ds(PAD + 8 * g, 8), :]
                north = fld[now, c, p, pl.ds(PAD + 8 * g + 1, 8), :]
                south = fld[now, c, p, pl.ds(PAD + 8 * g - 1, 8), :]
                place = p * groups + g
                east = outof(x, from_east, 127, place)
                west = outof(x, from_west, 0, place)
                new = (d - 4.0 * k) * x + (pa + k) * west + (ma + k) * east + (pb + k) * south + (mb + k) * north
                fresh.append((p, g, new))
                first = into(first, new, 0, place)
                last = into(last, new, 127, place)
        for p, g, new in fresh:
            fld[later, c, p, pl.ds(PAD + 8 * g, 8), :] = new

        @pl.when(s < steps - 1)
        def _():
            for p in range(nf):
                sbuf[0, after, c, NORTH, p, :] = fld[later, c, p, PAD, :]
                sbuf[0, after, c, SOUTH, p, :] = fld[later, c, p, PAD + rows - 1, :]
            sbuf[0, after, c, EAST] = first
            sbuf[0, after, c, WEST] = last
            start_halo(0, after, c)

    loop(steps, lambda s: loop(nlev, lambda c: forward(s, c)))
    moved = fld.at[steps % 2]

    def products(y, w, k, slot, c, p, g):
        pa, ma, pb, mb, d = w
        g_east, g_west = (pa + k) * y, (ma + k) * y
        here = pl.ds(PAD + 8 * g, 8)
        grd[slot, 0, c, p, here, :] = g_east
        grd[slot, 1, c, p, here, :] = g_west
        grd[slot, 2, c, p, here, :] = (pb + k) * y
        grd[slot, 3, c, p, here, :] = (mb + k) * y
        grd[slot, 4, c, p, here, :] = (d - 4.0 * k) * y
        return g_east, g_west

    def ship(t, slot, c, first, last):
        for p in range(nf):
            sbuf[1, t, c, NORTH, p, :] = grd[slot, 2, c, p, PAD, :]
            sbuf[1, t, c, SOUTH, p, :] = grd[slot, 3, c, p, PAD + rows - 1, :]
        sbuf[1, t, c, EAST] = first
        sbuf[1, t, c, WEST] = last
        start_halo(1, t, c)

    brought[3].wait()
    brought[4].wait()

    def adjoint_first(c):
        @pl.when(has_next)
        def _():
            wcopy(0, c).wait_recv()

        first, last = zero_tile, zero_tile
        start = {}
        for g in range(groups):
            for p in range(nf):
                y = -foll[c, p, span(g), :]
                for o in range(nobs):
                    y = y + wgt[o, p, c] * obs[0, o, span(g), :]
                start[p, g] = y
        for g in range(groups):
            w = winds(steps - 1, c, g)
            for p in range(nf):
                g_east, g_west = products(start[p, g], w, diff[p, c], 0, c, p, g)
                first = into(first, g_east, 0, p * groups + g)
                last = into(last, g_west, 127, p * groups + g)
        ship(0, 0, c, first, last)

    loop(nlev, adjoint_first)

    def gathered(t, slot, c, p, g, from_east, from_west):
        here = pl.ds(PAD + 8 * g, 8)
        place = p * groups + g
        east = outof(grd[slot, 0, c, p, here, :], from_east, 127, place)
        west = outof(grd[slot, 1, c, p, here, :], from_west, 0, place)
        north = grd[slot, 2, c, p, pl.ds(PAD + 8 * g + 1, 8), :]
        south = grd[slot, 3, c, p, pl.ds(PAD + 8 * g - 1, 8), :]
        return grd[slot, 4, c, p, here, :] + ((east + west) + (north + south))

    def receive(t, slot, c):
        wait_halo(1, t, c)
        north_row, south_row = edge_rows(1, t, c)
        for p in range(nf):
            grd[slot, 2, c, p, PAD + rows, :] = north_row[p]
            grd[slot, 3, c, p, PAD - 1, :] = south_row[p]
        return rbuf[1, t, c, EAST], rbuf[1, t, c, WEST]

    def adjoint(t, c):
        slot, other = lax.rem(t, 2), lax.rem(t + 1, 2)
        from_east, from_west = receive(t, slot, c)
        first, last = zero_tile, zero_tile
        start = {
            (p, g): gathered(t, slot, c, p, g, from_east, from_west)
            for g in range(groups) for p in range(nf)}
        for g in range(groups):
            w = winds(steps - 2 - t, c, g)
            for p in range(nf):
                g_east, g_west = products(start[p, g], w, diff[p, c], other, c, p, g)
                first = into(first, g_east, 0, p * groups + g)
                last = into(last, g_west, 127, p * groups + g)
        ship(t + 1, other, c, first, last)

    loop(steps - 1, lambda t: loop(nlev, lambda c: adjoint(t, c)))

    def adjoint_last(c):
        slot = (steps - 1) % 2
        from_east, from_west = receive(steps - 1, slot, c)
        done = {
            (p, g): gathered(steps - 1, slot, c, p, g, from_east, from_west)
            for g in range(groups) for p in range(nf)}
        for (p, g), y in done.items():
            back[c, p, span(g), :] = y

        @pl.when(win == nwin - 1)
        def _():
            pls[c] = dual[0, :, c] + back[c]
            if nwin > 1:
                wcopy(1, c).start()

    brought[5].wait()
    loop(nlev, adjoint_last)
    brought[6].wait()
    brought[7].wait()

    def fold(x):
        return jnp.sum(x.reshape(-1, 8, 128), axis=0)

    def observe(c, carry):
        return tuple(
            sum((wgt[o, p, c] * moved[c, p, pl.ds(PAD, rows), :] for p in range(nf)), carry[o])
            for o in range(nobs))

    ends = lax.fori_loop(0, nlev, observe, tuple(jnp.zeros((rows, 128), jnp.float32) for _ in range(nobs)))
    wv0, vv0 = zero_tile, zero_tile
    for o in range(nobs):
        v = obs[0, o]
        pm = (ov[0, o] * v + ends[o]) / ov[0, o]
        oend[o] = pm
        wv0 = wv0 + fold(pm * v)
        vv0 = vv0 + fold(v * v)

    def squares(c, acc):
        return acc + fold(dual[0, :, c] * dual[0, :, c]) + fold(inc[0, :, c] * inc[0, :, c])

    vv = lax.fori_loop(0, nlev, squares, vv0)

    def suffix(c, acc):
        @pl.when(has_next)
        def _():
            wcopy(1, c).wait_recv()
            pls[c] = dual[0, :, c] + back[c] + plin[c]

        @pl.when(has_next & has_prev)
        def _():
            wcopy(1, c).start()

        lam = dual[0, :, c]
        new = pls[c]
        base = mv[0, :, c] * (lam - new) + inc[0, :, c]
        pxs[c] = base

        @pl.when((win == 0) & has_next)
        def _():
            gout[c] = base - moved[c, :, pl.ds(PAD, rows), :]
            wcopy(2, c).start()

        return acc + fold(new * lam)

    wv = lax.fori_loop(0, nlev, suffix, wv0)

    def prefix(c, acc):
        @pl.when(has_prev)
        def _():
            wcopy(2, c).wait_recv()
            pxs[c] = pxs[c] + gin[c]

        @pl.when(has_prev & has_next)
        def _():
            gout[c] = pxs[c] - moved[c, :, pl.ds(PAD, rows), :]
            wcopy(2, c).start()

        return acc + fold(pxs[c] * inc[0, :, c])

    wv = lax.fori_loop(0, nlev, prefix, wv)

    def total(x):
        return jnp.broadcast_to(jnp.sum(jnp.sum(x, axis=0, keepdims=True), axis=1, keepdims=True), (1, 128))

    def ratio(a, b):
        return jnp.where(b > 0.0, a / jnp.where(b > 0.0, b, 1.0), 0.0)

    wv, vv = total(wv), total(vv)
    h = ratio(wv, vv)

    def residual(c, acc):
        a = pls[c] - h[None] * dual[0, :, c]
        b = pxs[c] - h[None] * inc[0, :, c]
        return acc + fold(a * a) + fold(b * b)

    uu = zero_tile
    for o in range(nobs):
        r = oend[o] - h * obs[0, o]
        uu = uu + fold(r * r)
    uu = total(lax.fori_loop(0, nlev, residual, uu))

    at = 0
    for index, (name, n, me) in enumerate(axes):
        mine = red.at[at + me]
        red[at + me, 0:1, :] = uu
        red[at + me, 1:2, :] = wv
        red[at + me, 2:3, :] = vv

        def swap(j, name=name, n=n, me=me, at=at):
            return pltpu.make_async_remote_copy(
                src_ref=red.at[at + me], dst_ref=red.at[at + me],
                send_sem=r_send.at[at + j], recv_sem=r_recv.at[at + j],
                device_id={name: lax.rem(me + j, n)}, device_id_type=MESH)

        for j in range(1, n):
            swap(j).start()
        for j in range(1, n):
            swap(j).wait_recv()
        parts = [tuple(red[at + i, q:q + 1, :] for q in range(3)) for i in range(n)]
        wv = functools.reduce(lambda a, b: a + b, [q[1] for q in parts])
        vv = functools.reduce(lambda a, b: a + b, [q[2] for q in parts])
        h = ratio(wv, vv)
        uu = functools.reduce(
            lambda a, b: a + b, [q[0] + (ratio(q[1], q[2]) - h) * (ratio(q[1], q[2]) - h) * q[2] for q in parts])
        for j in range(1, n):
            swap(j).wait_send()
        at += n

    h = wv / vv
    scale = jnp.sqrt(uu / count + 1e-06)
    inv = 1.0 / scale
    o_co[0] = jnp.sum(jnp.where(lane[0:1] == 0, h, 0.0))
    o_co[1] = jnp.sum(jnp.where(lane[0:1] == 0, scale, 0.0))

    def finish(c):
        o_lam[0, :, c] = (pls[c] - h[None] * dual[0, :, c]) * inv[None]
        o_inc[0, :, c] = (pxs[c] - h[None] * inc[0, :, c]) * inv[None]

    loop(nlev, finish)
    for o in range(nobs):
        o_obs[0, o] = (oend[o] - h * obs[0, o]) * inv

    for kind in range(2):
        pltpu.make_async_remote_copy(
            src_ref=sbuf.at[kind], dst_ref=rbuf.at[kind], send_sem=h_send.at[kind],
            recv_sem=h_recv.at[kind, 0, 0], device_id=to[0], device_id_type=MESH).wait_send()

    def settle(c):
        @pl.when(has_prev)
        def _():
            wcopy(0, c).wait_send()
            wcopy(1, c).wait_send()

        @pl.when(has_next)
        def _():
            wcopy(2, c).wait_send()

    loop(nlev, settle)


def per_device(mesh, dual, obs_dual, increment, trajectory, diffusion, obs_weight, model_var, obs_var):
    nwin, ntx, nty = (mesh.shape[a] for a in ("win", "tx", "ty"))
    _, nf, nlev, rows, cols = dual.shape
    nobs, steps = obs_dual.shape[1], trajectory.shape[1]
    assert cols == 128 and rows % 8 == 0 and nf * rows // 8 <= 128 and nf <= 8
    count = (2 * nf * nlev + nobs) * rows * cols * nwin * ntx * nty
    sizes = (nwin, ntx, nty, steps, nf, nlev, rows, nobs, float(count))
    vmem, smem = pl.BlockSpec(memory_space=pltpu.VMEM), pl.BlockSpec(memory_space=pltpu.SMEM)
    chunks = pltpu.VMEM((nlev, nf, rows, cols), jnp.float32)
    messages = pltpu.VMEM((2, steps, nlev, 4, 8, cols), jnp.float32)
    n_red = nwin + ntx + nty
    return pl.pallas_call(
        functools.partial(kernel, sizes),
        out_shape=(
            jax.ShapeDtypeStruct(dual.shape, jnp.float32),
            jax.ShapeDtypeStruct(obs_dual.shape, jnp.float32),
            jax.ShapeDtypeStruct(increment.shape, jnp.float32),
            jax.ShapeDtypeStruct((2,), jnp.float32),
        ),
        in_specs=[pl.BlockSpec(memory_space=pltpu.HBM)] * 8,
        out_specs=(vmem, vmem, vmem, smem),
        scratch_shapes=[
            pltpu.VMEM(dual.shape, jnp.float32), pltpu.VMEM(obs_dual.shape, jnp.float32),
            pltpu.VMEM(increment.shape, jnp.float32), pltpu.VMEM(trajectory.shape, jnp.float32),
            pltpu.VMEM(model_var.shape, jnp.float32), pltpu.VMEM(obs_var.shape, jnp.float32),
            pltpu.SMEM(diffusion.shape, jnp.float32), pltpu.SMEM(obs_weight.shape, jnp.float32),
            pltpu.SemaphoreType.DMA((8,)),
            pltpu.VMEM((2, nlev, nf, rows + 2 * PAD, cols), jnp.float32),
            pltpu.VMEM((2, 5, nlev, nf, rows + 2 * PAD, cols), jnp.float32),
            chunks, chunks, chunks, chunks, chunks, chunks, chunks,
            pltpu.VMEM((nobs, rows, cols), jnp.float32),
            messages, messages,
            pltpu.VMEM((n_red, 8, cols), jnp.float32),
            pltpu.SemaphoreType.DMA((2,)),
            pltpu.SemaphoreType.DMA((2, steps, nlev)),
            pltpu.SemaphoreType.DMA((3, nlev)),
            pltpu.SemaphoreType.DMA((3, nlev)),
            pltpu.SemaphoreType.DMA((n_red,)),
            pltpu.SemaphoreType.DMA((n_red,)),
        ],
        compiler_params=pltpu.CompilerParams(
            collective_id=0, has_side_effects=True, vmem_limit_bytes=48 * 1024 * 1024),
    )(dual, obs_dual, increment, trajectory, model_var, obs_var, diffusion, obs_weight)


def solution(mesh):
    in_specs = (
        P("win", None, None, "ty", "tx"),
        P("win", None, "ty", "tx"),
        P("win", None, None, "ty", "tx"),
        P("win", None, None, None, "ty", "tx"),
        P(),
        P(),
        P("win", None, None, "ty", "tx"),
        P("win", None, "ty", "tx"),
    )
    out_specs = (
        P("win", None, None, "ty", "tx"),
        P("win", None, "ty", "tx"),
        P("win", None, None, "ty", "tx"),
        P(),
    )
    return jax.shard_map(
        functools.partial(per_device, mesh), mesh=mesh, in_specs=in_specs, out_specs=out_specs, check_vma=False
    )
```

```python
import functools
import jax
import jax.numpy as jnp
from jax import lax
from jax.experimental import pallas as pl
from jax.experimental.pallas import tpu as pltpu
from jax.sharding import PartitionSpec as P

MESH = pl.DeviceIdType.MESH
PAD = 8
EAST, WEST, NORTH, SOUTH = range(4)


def kernel(sizes, h_dual, h_obs, h_inc, h_traj, h_mv, h_ov, h_diff, h_wgt,
           o_lam, o_obs, o_inc, o_co,
           dual, obs, inc, traj, mv, ov, diff, wgt, i_sem,
           fld, grd, back, foll, plin, pls, pxs, gin, gout, oend, sbuf, rbuf, red,
           h_send, h_recv, w_send, w_recv, r_send, r_recv):
    nwin, ntx, nty, steps, nf, nlev, rows, nobs, count = sizes
    groups = rows // 8
    win, tx, ty = lax.axis_index("win"), lax.axis_index("tx"), lax.axis_index("ty")
    has_prev, has_next = win > 0, win < nwin - 1
    right, left = lax.rem(tx + 1, ntx), lax.rem(tx + ntx - 1, ntx)
    lane = lax.broadcasted_iota(jnp.int32, (8, 128), 1)
    axes = (("ty", nty, ty), ("tx", ntx, tx), ("win", nwin, win))

    brought = [
        pltpu.make_async_copy(src, dst, i_sem.at[i])
        for i, (src, dst) in enumerate((
            (h_inc, inc), (h_diff, diff), (h_traj, traj), (h_obs, obs),
            (h_wgt, wgt), (h_dual, dual), (h_mv, mv), (h_ov, ov)))
    ]
    for copy in brought:
        copy.start()

    barrier = pltpu.get_barrier_semaphore()
    for name, n, me in axes:
        for j in range(1, n):
            pl.semaphore_signal(barrier, inc=1, device_id={name: lax.rem(me + j, n)}, device_id_type=MESH)

    @pl.when(win == nwin - 1)
    def _():
        foll[...] = jnp.zeros(foll.shape, jnp.float32)
        plin[...] = jnp.zeros(plin.shape, jnp.float32)

    pl.semaphore_wait(barrier, (nty - 1) + (ntx - 1) + (nwin - 1))

    north_of, south_of = lax.rem(ty + 1, nty), lax.rem(ty + nty - 1, nty)
    to = ({"tx": left}, {"tx": right}, {"ty": south_of}, {"ty": north_of})

    def start_halo(kind, s, c):
        for side in range(4):
            pltpu.make_async_remote_copy(
                src_ref=sbuf.at[kind, s, c, side], dst_ref=rbuf.at[kind, s, c, side],
                send_sem=h_send.at[kind], recv_sem=h_recv.at[kind, s, c],
                device_id=to[side], device_id_type=MESH).start()

    def wait_halo(kind, s, c):
        pltpu.make_async_remote_copy(
            src_ref=sbuf.at[kind, s, c], dst_ref=rbuf.at[kind, s, c],
            send_sem=h_send.at[kind], recv_sem=h_recv.at[kind, s, c],
            device_id=to[0], device_id_type=MESH).wait_recv()

    def edge_rows(kind, s, c):
        north = jnp.where(ty == nty - 1, 0.0, rbuf[kind, s, c, NORTH])
        south = jnp.where(ty == 0, 0.0, rbuf[kind, s, c, SOUTH])
        return north, south

    def wcopy(what, c):
        src, dst, to = (
            (h_dual.at[0, :, c], foll.at[c], win - 1),
            (pls.at[c], plin.at[c], win - 1),
            (gout.at[c], gin.at[c], win + 1),
        )[what]
        return pltpu.make_async_remote_copy(
            src_ref=src, dst_ref=dst, send_sem=w_send.at[what, c], recv_sem=w_recv.at[what, c],
            device_id={"win": to}, device_id_type=MESH)

    @pl.when(has_prev)
    def _():
        for c in range(nlev):
            wcopy(0, c).start()

    def loop(n, body):
        def step(i, carry):
            body(i)
            return carry
        lax.fori_loop(0, n, step, 0)

    def span(g):
        return pl.ds(8 * g, 8)

    def winds(s, c, g):
        a, b = traj[0, s, 0, c, span(g), :], traj[0, s, 1, c, span(g), :]
        pa, pb = jnp.maximum(a, 0.0), jnp.maximum(b, 0.0)
        ma, mb = pa - a, pb - b
        return pa, ma, pb, mb, 1.0 - ((pa + ma) + (pb + mb))

    pair = lane >> 1

    def into(acc, value, k):
        return jnp.where(pair == k, pltpu.roll(value, 2 * k + 1, 1), acc)

    def edge_columns(kind, s, c):
        return jnp.where(
            lane == 2 * pair, pltpu.roll(rbuf[kind, s, c, EAST], 127, 1), pltpu.roll(rbuf[kind, s, c, WEST], 1, 1))

    def shifted(for_east, for_west, columns, k):
        edge = pltpu.roll(columns, (127 - 2 * k) % 128, 1)
        east = jnp.where(lane == 127, edge, pltpu.roll(for_east, 127, 1))
        west = jnp.where(lane == 0, edge, pltpu.roll(for_west, 1, 1))
        return east, west

    zero_tile = jnp.zeros((8, 128), jnp.float32)

    def forward_first(c):
        packed = zero_tile
        for p in range(nf):
            for g in range(groups):
                value = inc[0, p, c, span(g), :]
                fld[0, c, p, pl.ds(PAD + 8 * g, 8), :] = value
                packed = into(packed, value, p * groups + g)
            sbuf[0, 0, c, NORTH, p, :] = inc[0, p, c, 0, :]
            sbuf[0, 0, c, SOUTH, p, :] = inc[0, p, c, rows - 1, :]
        sbuf[0, 0, c, EAST] = packed
        sbuf[0, 0, c, WEST] = packed
        start_halo(0, 0, c)


    def forward(s, c):
        wait_halo(0, s, c)
        now, later = lax.rem(s, 2), lax.rem(s + 1, 2)
        north_row, south_row = edge_rows(0, s, c)
        for p in range(nf):
            fld[now, c, p, PAD - 1, :] = south_row[p]
            fld[now, c, p, PAD + rows, :] = north_row[p]
        columns = edge_columns(0, s, c)
        packed = zero_tile
        ks = [diff[p, c] for p in range(nf)]
        after = jnp.minimum(s + 1, steps - 1)
        fresh = []
        for g in range(groups):
            pa, ma, pb, mb, d = winds(s, c, g)
            for p in range(nf):
                k = ks[p]
                x = fld[now, c, p, pl.ds(PAD + 8 * g, 8), :]
                north = fld[now, c, p, pl.ds(PAD + 8 * g + 1, 8), :]
                south = fld[now, c, p, pl.ds(PAD + 8 * g - 1, 8), :]
                place = p * groups + g
                east, west = shifted(x, x, columns, place)
                new = (d - 4.0 * k) * x + (pa + k) * west + (ma + k) * east + (pb + k) * south + (mb + k) * north
                fresh.append((p, g, new))
                packed = into(packed, new, place)
        for p, g, new in fresh:
            fld[later, c, p, pl.ds(PAD + 8 * g, 8), :] = new

        @pl.when(s < steps - 1)
        def _():
            for p in range(nf):
                sbuf[0, after, c, NORTH, p, :] = fld[later, c, p, PAD, :]
                sbuf[0, after, c, SOUTH, p, :] = fld[later, c, p, PAD + rows - 1, :]
            sbuf[0, after, c, EAST] = packed
            sbuf[0, after, c, WEST] = packed
            start_halo(0, after, c)

    moved = fld.at[steps % 2]

    def products(y, w, k, slot, c, p, g):
        pa, ma, pb, mb, d = w
        g_east, g_west = (pa + k) * y, (ma + k) * y
        here = pl.ds(PAD + 8 * g, 8)
        grd[slot, 0, c, p, here, :] = g_east
        grd[slot, 1, c, p, here, :] = g_west
        grd[slot, 2, c, p, here, :] = (pb + k) * y
        grd[slot, 3, c, p, here, :] = (mb + k) * y
        grd[slot, 4, c, p, here, :] = (d - 4.0 * k) * y
        return jnp.where(lane == 0, g_east, g_west)

    def ship(t, slot, c, packed):
        for p in range(nf):
            sbuf[1, t, c, NORTH, p, :] = grd[slot, 2, c, p, PAD, :]
            sbuf[1, t, c, SOUTH, p, :] = grd[slot, 3, c, p, PAD + rows - 1, :]
        sbuf[1, t, c, EAST] = packed
        sbuf[1, t, c, WEST] = packed
        start_halo(1, t, c)

    def adjoint_first(c):
        @pl.when(has_next)
        def _():
            wcopy(0, c).wait_recv()

        packed = zero_tile
        ks = [diff[p, c] for p in range(nf)]
        ws = [[wgt[o, p, c] for o in range(nobs)] for p in range(nf)]
        start = {}
        for g in range(groups):
            observed = [obs[0, o, span(g), :] for o in range(nobs)]
            for p in range(nf):
                y = -foll[c, p, span(g), :]
                for o in range(nobs):
                    y = y + ws[p][o] * observed[o]
                start[p, g] = y
        for g in range(groups):
            w = winds(steps - 1, c, g)
            for p in range(nf):
                packed = into(packed, products(start[p, g], w, ks[p], 0, c, p, g), p * groups + g)
        ship(0, 0, c, packed)


    def gathered(slot, c, p, g, columns):
        here = pl.ds(PAD + 8 * g, 8)
        east, west = shifted(grd[slot, 0, c, p, here, :], grd[slot, 1, c, p, here, :], columns, p * groups + g)
        north = grd[slot, 2, c, p, pl.ds(PAD + 8 * g + 1, 8), :]
        south = grd[slot, 3, c, p, pl.ds(PAD + 8 * g - 1, 8), :]
        return grd[slot, 4, c, p, here, :] + ((east + west) + (north + south))

    def receive(t, slot, c):
        wait_halo(1, t, c)
        north_row, south_row = edge_rows(1, t, c)
        for p in range(nf):
            grd[slot, 2, c, p, PAD + rows, :] = north_row[p]
            grd[slot, 3, c, p, PAD - 1, :] = south_row[p]
        return edge_columns(1, t, c)

    def adjoint(t, c):
        slot, other = lax.rem(t, 2), lax.rem(t + 1, 2)
        columns = receive(t, slot, c)
        packed = zero_tile
        ks = [diff[p, c] for p in range(nf)]
        start = {
            (p, g): gathered(slot, c, p, g, columns)
            for g in range(groups) for p in range(nf)}
        for g in range(groups):
            w = winds(steps - 2 - t, c, g)
            for p in range(nf):
                packed = into(packed, products(start[p, g], w, ks[p], other, c, p, g), p * groups + g)
        ship(t + 1, other, c, packed)


    def adjoint_last(c):
        slot = (steps - 1) % 2
        columns = receive(steps - 1, slot, c)
        done = {
            (p, g): gathered(slot, c, p, g, columns)
            for g in range(groups) for p in range(nf)}
        for (p, g), y in done.items():
            back[c, p, span(g), :] = y

        @pl.when(win == nwin - 1)
        def _():
            pls[c] = dual[0, :, c] + back[c]
            if nwin > 1:
                wcopy(1, c).start()

    for copy in brought:
        copy.wait()

    def model(stage):
        now = lax.rem(stage + jnp.where(win == nwin - 1, 1, 0), 2)

        @pl.when(now == 0)
        def _():
            loop(nlev, forward_first)
            loop(steps, lambda s: loop(nlev, lambda c: forward(s, c)))

        @pl.when(now == 1)
        def _():
            loop(nlev, adjoint_first)
            loop(steps - 1, lambda t: loop(nlev, lambda c: adjoint(t, c)))
            loop(nlev, adjoint_last)

    loop(2, model)

    def fold(x):
        return jnp.sum(x.reshape(-1, 8, 128), axis=0)

    def observe(c, carry):
        return tuple(
            sum((wgt[o, p, c] * moved[c, p, pl.ds(PAD, rows), :] for p in range(nf)), carry[o])
            for o in range(nobs))

    ends = lax.fori_loop(0, nlev, observe, tuple(jnp.zeros((rows, 128), jnp.float32) for _ in range(nobs)))
    wv0, vv0 = zero_tile, zero_tile
    for o in range(nobs):
        v = obs[0, o]
        pm = (ov[0, o] * v + ends[o]) / ov[0, o]
        oend[o] = pm
        wv0 = wv0 + fold(pm * v)
        vv0 = vv0 + fold(v * v)

    def squares(c, acc):
        return acc + fold(dual[0, :, c] * dual[0, :, c]) + fold(inc[0, :, c] * inc[0, :, c])

    vv = lax.fori_loop(0, nlev, squares, vv0)

    def suffix(c, acc):
        @pl.when(has_next)
        def _():
            wcopy(1, c).wait_recv()
            pls[c] = dual[0, :, c] + back[c] + plin[c]

        @pl.when(has_next & has_prev)
        def _():
            wcopy(1, c).start()

        lam = dual[0, :, c]
        new = pls[c]
        base = mv[0, :, c] * (lam - new) + inc[0, :, c]
        pxs[c] = base

        @pl.when((win == 0) & has_next)
        def _():
            gout[c] = base - moved[c, :, pl.ds(PAD, rows), :]
            wcopy(2, c).start()

        return acc + fold(new * lam)

    wv = lax.fori_loop(0, nlev, suffix, wv0)

    def prefix(c, acc):
        @pl.when(has_prev)
        def _():
            wcopy(2, c).wait_recv()
            pxs[c] = pxs[c] + gin[c]

        @pl.when(has_prev & has_next)
        def _():
            gout[c] = pxs[c] - moved[c, :, pl.ds(PAD, rows), :]
            wcopy(2, c).start()

        return acc + fold(pxs[c] * inc[0, :, c])

    wv = lax.fori_loop(0, nlev, prefix, wv)

    def total(x):
        return jnp.broadcast_to(jnp.sum(jnp.sum(x, axis=0, keepdims=True), axis=1, keepdims=True), (1, 128))

    def ratio(a, b):
        return jnp.where(b > 0.0, a / jnp.where(b > 0.0, b, 1.0), 0.0)

    wv, vv = total(wv), total(vv)
    h = ratio(wv, vv)

    def residual(c, acc):
        a = pls[c] - h[None] * dual[0, :, c]
        b = pxs[c] - h[None] * inc[0, :, c]
        return acc + fold(a * a) + fold(b * b)

    uu = zero_tile
    for o in range(nobs):
        r = oend[o] - h * obs[0, o]
        uu = uu + fold(r * r)
    uu = total(lax.fori_loop(0, nlev, residual, uu))

    at = 0
    for index, (name, n, me) in enumerate(axes):
        mine = red.at[at + me]
        red[at + me, 0:1, :] = uu
        red[at + me, 1:2, :] = wv
        red[at + me, 2:3, :] = vv

        def swap(j, name=name, n=n, me=me, at=at):
            return pltpu.make_async_remote_copy(
                src_ref=red.at[at + me], dst_ref=red.at[at + me],
                send_sem=r_send.at[at + j], recv_sem=r_recv.at[at + j],
                device_id={name: lax.rem(me + j, n)}, device_id_type=MESH)

        for j in range(1, n):
            swap(j).start()
        for j in range(1, n):
            swap(j).wait_recv()
        parts = [tuple(red[at + i, q:q + 1, :] for q in range(3)) for i in range(n)]
        wv = functools.reduce(lambda a, b: a + b, [q[1] for q in parts])
        vv = functools.reduce(lambda a, b: a + b, [q[2] for q in parts])
        h = ratio(wv, vv)
        uu = functools.reduce(
            lambda a, b: a + b, [q[0] + (ratio(q[1], q[2]) - h) * (ratio(q[1], q[2]) - h) * q[2] for q in parts])
        for j in range(1, n):
            swap(j).wait_send()
        at += n

    h = wv / vv
    scale = jnp.sqrt(uu / count + 1e-06)
    inv = 1.0 / scale
    o_co[0] = jnp.sum(jnp.where(lane[0:1] == 0, h, 0.0))
    o_co[1] = jnp.sum(jnp.where(lane[0:1] == 0, scale, 0.0))

    def finish(c):
        o_lam[0, :, c] = (pls[c] - h[None] * dual[0, :, c]) * inv[None]
        o_inc[0, :, c] = (pxs[c] - h[None] * inc[0, :, c]) * inv[None]

    loop(nlev, finish)
    for o in range(nobs):
        o_obs[0, o] = (oend[o] - h * obs[0, o]) * inv

    for kind in range(2):
        pltpu.make_async_remote_copy(
            src_ref=sbuf.at[kind], dst_ref=rbuf.at[kind], send_sem=h_send.at[kind],
            recv_sem=h_recv.at[kind, 0, 0], device_id=to[0], device_id_type=MESH).wait_send()

    def settle(c):
        @pl.when(has_prev)
        def _():
            wcopy(0, c).wait_send()
            wcopy(1, c).wait_send()

        @pl.when(has_next)
        def _():
            wcopy(2, c).wait_send()

    loop(nlev, settle)


def per_device(mesh, dual, obs_dual, increment, trajectory, diffusion, obs_weight, model_var, obs_var):
    nwin, ntx, nty = (mesh.shape[a] for a in ("win", "tx", "ty"))
    _, nf, nlev, rows, cols = dual.shape
    nobs, steps = obs_dual.shape[1], trajectory.shape[1]
    assert cols == 128 and rows % 8 == 0 and nf * rows // 4 <= 128 and nf <= 8
    count = (2 * nf * nlev + nobs) * rows * cols * nwin * ntx * nty
    sizes = (nwin, ntx, nty, steps, nf, nlev, rows, nobs, float(count))
    vmem, smem = pl.BlockSpec(memory_space=pltpu.VMEM), pl.BlockSpec(memory_space=pltpu.SMEM)
    chunks = pltpu.VMEM((nlev, nf, rows, cols), jnp.float32)
    messages = pltpu.VMEM((2, steps, nlev, 4, 8, cols), jnp.float32)
    n_red = nwin + ntx + nty
    return pl.pallas_call(
        functools.partial(kernel, sizes),
        out_shape=(
            jax.ShapeDtypeStruct(dual.shape, jnp.float32),
            jax.ShapeDtypeStruct(obs_dual.shape, jnp.float32),
            jax.ShapeDtypeStruct(increment.shape, jnp.float32),
            jax.ShapeDtypeStruct((2,), jnp.float32),
        ),
        in_specs=[pl.BlockSpec(memory_space=pltpu.HBM)] * 8,
        out_specs=(vmem, vmem, vmem, smem),
        scratch_shapes=[
            pltpu.VMEM(dual.shape, jnp.float32), pltpu.VMEM(obs_dual.shape, jnp.float32),
            pltpu.VMEM(increment.shape, jnp.float32), pltpu.VMEM(trajectory.shape, jnp.float32),
            pltpu.VMEM(model_var.shape, jnp.float32), pltpu.VMEM(obs_var.shape, jnp.float32),
            pltpu.SMEM(diffusion.shape, jnp.float32), pltpu.SMEM(obs_weight.shape, jnp.float32),
            pltpu.SemaphoreType.DMA((8,)),
            pltpu.VMEM((2, nlev, nf, rows + 2 * PAD, cols), jnp.float32),
            pltpu.VMEM((2, 5, nlev, nf, rows + 2 * PAD, cols), jnp.float32),
            chunks, chunks, chunks, chunks, chunks, chunks, chunks,
            pltpu.VMEM((nobs, rows, cols), jnp.float32),
            messages, messages,
            pltpu.VMEM((n_red, 8, cols), jnp.float32),
            pltpu.SemaphoreType.DMA((2,)),
            pltpu.SemaphoreType.DMA((2, steps, nlev)),
            pltpu.SemaphoreType.DMA((3, nlev)),
            pltpu.SemaphoreType.DMA((3, nlev)),
            pltpu.SemaphoreType.DMA((n_red,)),
            pltpu.SemaphoreType.DMA((n_red,)),
        ],
        compiler_params=pltpu.CompilerParams(
            collective_id=0, has_side_effects=True, vmem_limit_bytes=60 * 1024 * 1024),
    )(dual, obs_dual, increment, trajectory, model_var, obs_var, diffusion, obs_weight)


def solution(mesh):
    in_specs = (
        P("win", None, None, "ty", "tx"),
        P("win", None, "ty", "tx"),
        P("win", None, None, "ty", "tx"),
        P("win", None, None, None, "ty", "tx"),
        P(),
        P(),
        P("win", None, None, "ty", "tx"),
        P("win", None, "ty", "tx"),
    )
    out_specs = (
        P("win", None, None, "ty", "tx"),
        P("win", None, "ty", "tx"),
        P("win", None, None, "ty", "tx"),
        P(),
    )
    return jax.shard_map(
        functools.partial(per_device, mesh), mesh=mesh, in_specs=in_specs, out_specs=out_specs, check_vma=False
    )
```

```python
import functools
import jax
import jax.numpy as jnp
from jax import lax
from jax.experimental import pallas as pl
from jax.experimental.pallas import tpu as pltpu
from jax.sharding import PartitionSpec as P

MESH = pl.DeviceIdType.MESH
PAD = 8
EAST, WEST, NORTH, SOUTH = range(4)


def kernel(sizes, h_dual, h_obs, h_inc, h_traj, h_mv, h_ov, h_diff, h_wgt,
           o_lam, o_obs, o_inc, o_co,
           dual, obs, inc, traj, mv, ov, diff, wgt, i_sem,
           fld, grd, back, foll, plin, pls, pxs, gin, gout, oend, sbuf, rbuf, red,
           wsum, h_send, h_recv, w_send, w_recv, r_send, r_recv):
    nwin, ntx, nty, steps, nf, nlev, rows, nobs, count = sizes
    groups = rows // 8
    win, tx, ty = lax.axis_index("win"), lax.axis_index("tx"), lax.axis_index("ty")
    has_prev, has_next = win > 0, win < nwin - 1
    right, left = lax.rem(tx + 1, ntx), lax.rem(tx + ntx - 1, ntx)
    lane = lax.broadcasted_iota(jnp.int32, (8, 128), 1)
    is_last = (win == nwin - 1) & has_prev
    rounds = (
        (tx, ntx, [{"tx": lax.rem(tx + j, ntx)} for j in range(1, ntx)]),
        (ty * nwin + win, nty * nwin, [
            {"ty": lax.rem(ty + j // nwin, nty), "win": lax.rem(win + j % nwin, nwin)}
            for j in range(1, nty * nwin)]),
    )

    brought = [
        pltpu.make_async_copy(src, dst, i_sem.at[i])
        for i, (src, dst) in enumerate((
            (h_inc, inc), (h_diff, diff), (h_traj, traj), (h_obs, obs),
            (h_wgt, wgt), (h_dual, dual), (h_mv, mv), (h_ov, ov)))
    ]
    for copy in brought:
        copy.start()

    barrier = pltpu.get_barrier_semaphore()
    for _, _, partners in rounds:
        for partner in partners:
            pl.semaphore_signal(barrier, inc=1, device_id=partner, device_id_type=MESH)

    @pl.when(win == nwin - 1)
    def _():
        foll[...] = jnp.zeros(foll.shape, jnp.float32)
        plin[...] = jnp.zeros(plin.shape, jnp.float32)

    pl.semaphore_wait(barrier, (ntx - 1) + (nty * nwin - 1))

    north_of, south_of = lax.rem(ty + 1, nty), lax.rem(ty + nty - 1, nty)
    to = ({"tx": left}, {"tx": right}, {"ty": south_of}, {"ty": north_of})

    def start_halo(kind, s, c):
        for side in range(4):
            pltpu.make_async_remote_copy(
                src_ref=sbuf.at[kind, s, c, side], dst_ref=rbuf.at[kind, s, c, side],
                send_sem=h_send.at[kind], recv_sem=h_recv.at[kind, s, c],
                device_id=to[side], device_id_type=MESH).start()

    def wait_halo(kind, s, c):
        pltpu.make_async_remote_copy(
            src_ref=sbuf.at[kind, s, c], dst_ref=rbuf.at[kind, s, c],
            send_sem=h_send.at[kind], recv_sem=h_recv.at[kind, s, c],
            device_id=to[0], device_id_type=MESH).wait_recv()

    def edge_rows(kind, s, c):
        north = jnp.where(ty == nty - 1, 0.0, rbuf[kind, s, c, NORTH])
        south = jnp.where(ty == 0, 0.0, rbuf[kind, s, c, SOUTH])
        return north, south

    def wcopy(what, c):
        src, dst, to = (
            (h_dual.at[0, :, c], foll.at[c], win - 1),
            (pls.at[c], plin.at[c], win - 1),
            (gout.at[c], gin.at[c], win + 1),
        )[what]
        return pltpu.make_async_remote_copy(
            src_ref=src, dst_ref=dst, send_sem=w_send.at[what, c], recv_sem=w_recv.at[what, c],
            device_id={"win": to}, device_id_type=MESH)

    @pl.when(has_prev)
    def _():
        for c in range(2):
            wcopy(0, c).start()

    @pl.when(has_prev & has_next)
    def _():
        for c in range(2, nlev):
            wcopy(0, c).start()

    def loop(n, body):
        def step(i, carry):
            body(i)
            return carry
        lax.fori_loop(0, n, step, 0)

    def span(g):
        return pl.ds(8 * g, 8)

    def winds(s, c, g):
        a, b = traj[0, s, 0, c, span(g), :], traj[0, s, 1, c, span(g), :]
        pa, pb = jnp.maximum(a, 0.0), jnp.maximum(b, 0.0)
        ma, mb = pa - a, pb - b
        return pa, ma, pb, mb, 1.0 - ((pa + ma) + (pb + mb))

    pair = lane >> 1

    def into(acc, value, k):
        return jnp.where(pair == k, pltpu.roll(value, 2 * k + 1, 1), acc)

    def edge_columns(kind, s, c):
        return jnp.where(
            lane == 2 * pair, pltpu.roll(rbuf[kind, s, c, EAST], 127, 1), pltpu.roll(rbuf[kind, s, c, WEST], 1, 1))

    def shifted(for_east, for_west, columns, k):
        edge = pltpu.roll(columns, (127 - 2 * k) % 128, 1)
        east = jnp.where(lane == 127, edge, pltpu.roll(for_east, 127, 1))
        west = jnp.where(lane == 0, edge, pltpu.roll(for_west, 1, 1))
        return east, west

    zero_tile = jnp.zeros((8, 128), jnp.float32)

    def forward_first(c):
        packed = zero_tile
        for p in range(nf):
            for g in range(groups):
                value = inc[0, p, c, span(g), :]
                fld[0, c, p, pl.ds(PAD + 8 * g, 8), :] = value
                packed = into(packed, value, p * groups + g)
            sbuf[0, 0, c, NORTH, p, :] = inc[0, p, c, 0, :]
            sbuf[0, 0, c, SOUTH, p, :] = inc[0, p, c, rows - 1, :]
        sbuf[0, 0, c, EAST] = packed
        sbuf[0, 0, c, WEST] = packed
        start_halo(0, 0, c)


    def forward(s, c):
        wait_halo(0, s, c)
        now, later = lax.rem(s, 2), lax.rem(s + 1, 2)
        north_row, south_row = edge_rows(0, s, c)
        for p in range(nf):
            fld[now, c, p, PAD - 1, :] = south_row[p]
            fld[now, c, p, PAD + rows, :] = north_row[p]
        columns = edge_columns(0, s, c)
        packed = zero_tile
        ks = [diff[p, c] for p in range(nf)]
        after = jnp.minimum(s + 1, steps - 1)
        fresh = []
        for g in range(groups):
            pa, ma, pb, mb, d = winds(s, c, g)
            for p in range(nf):
                k = ks[p]
                x = fld[now, c, p, pl.ds(PAD + 8 * g, 8), :]
                north = fld[now, c, p, pl.ds(PAD + 8 * g + 1, 8), :]
                south = fld[now, c, p, pl.ds(PAD + 8 * g - 1, 8), :]
                place = p * groups + g
                east, west = shifted(x, x, columns, place)
                new = (d - 4.0 * k) * x + (pa + k) * west + (ma + k) * east + (pb + k) * south + (mb + k) * north
                fresh.append((p, g, new))
                packed = into(packed, new, place)
        for p, g, new in fresh:
            fld[later, c, p, pl.ds(PAD + 8 * g, 8), :] = new

        @pl.when(s < steps - 1)
        def _():
            for p in range(nf):
                sbuf[0, after, c, NORTH, p, :] = fld[later, c, p, PAD, :]
                sbuf[0, after, c, SOUTH, p, :] = fld[later, c, p, PAD + rows - 1, :]
            sbuf[0, after, c, EAST] = packed
            sbuf[0, after, c, WEST] = packed
            start_halo(0, after, c)

    moved = fld.at[steps % 2]

    def products(y, w, k, slot, c, p, g):
        pa, ma, pb, mb, d = w
        g_east, g_west = (pa + k) * y, (ma + k) * y
        here = pl.ds(PAD + 8 * g, 8)
        grd[slot, 0, c, p, here, :] = g_east
        grd[slot, 1, c, p, here, :] = g_west
        grd[slot, 2, c, p, here, :] = (pb + k) * y
        grd[slot, 3, c, p, here, :] = (mb + k) * y
        grd[slot, 4, c, p, here, :] = (d - 4.0 * k) * y
        return jnp.where(lane == 0, g_east, g_west)

    def ship(t, slot, c, packed):
        for p in range(nf):
            sbuf[1, t, c, NORTH, p, :] = grd[slot, 2, c, p, PAD, :]
            sbuf[1, t, c, SOUTH, p, :] = grd[slot, 3, c, p, PAD + rows - 1, :]
        sbuf[1, t, c, EAST] = packed
        sbuf[1, t, c, WEST] = packed
        start_halo(1, t, c)

    def adjoint_first(c):
        @pl.when(has_next)
        def _():
            wcopy(0, c).wait_recv()

        packed = zero_tile
        ks = [diff[p, c] for p in range(nf)]
        ws = [[wgt[o, p, c] for o in range(nobs)] for p in range(nf)]
        start = {}
        for g in range(groups):
            observed = [obs[0, o, span(g), :] for o in range(nobs)]
            for p in range(nf):
                y = -foll[c, p, span(g), :]
                for o in range(nobs):
                    y = y + ws[p][o] * observed[o]
                start[p, g] = y
        for g in range(groups):
            w = winds(steps - 1, c, g)
            for p in range(nf):
                packed = into(packed, products(start[p, g], w, ks[p], 0, c, p, g), p * groups + g)
        ship(0, 0, c, packed)


    def gathered(slot, c, p, g, columns):
        here = pl.ds(PAD + 8 * g, 8)
        east, west = shifted(grd[slot, 0, c, p, here, :], grd[slot, 1, c, p, here, :], columns, p * groups + g)
        north = grd[slot, 2, c, p, pl.ds(PAD + 8 * g + 1, 8), :]
        south = grd[slot, 3, c, p, pl.ds(PAD + 8 * g - 1, 8), :]
        return grd[slot, 4, c, p, here, :] + ((east + west) + (north + south))

    def receive(t, slot, c):
        wait_halo(1, t, c)
        north_row, south_row = edge_rows(1, t, c)
        for p in range(nf):
            grd[slot, 2, c, p, PAD + rows, :] = north_row[p]
            grd[slot, 3, c, p, PAD - 1, :] = south_row[p]
        return edge_columns(1, t, c)

    def adjoint(t, c):
        slot, other = lax.rem(t, 2), lax.rem(t + 1, 2)
        columns = receive(t, slot, c)
        packed = zero_tile
        ks = [diff[p, c] for p in range(nf)]
        start = {
            (p, g): gathered(slot, c, p, g, columns)
            for g in range(groups) for p in range(nf)}
        for g in range(groups):
            w = winds(steps - 2 - t, c, g)
            for p in range(nf):
                packed = into(packed, products(start[p, g], w, ks[p], other, c, p, g), p * groups + g)
        ship(t + 1, other, c, packed)


    def adjoint_last(c):
        slot = (steps - 1) % 2
        columns = receive(steps - 1, slot, c)
        done = {
            (p, g): gathered(slot, c, p, g, columns)
            for g in range(groups) for p in range(nf)}
        for (p, g), y in done.items():
            back[c, p, span(g), :] = y
        pls[c] = dual[0, :, c] + back[c]

    def fold(x):
        return jnp.sum(x.reshape(-1, 8, 128), axis=0)

    def suffix(c):
        @pl.when(has_next)
        def _():
            wcopy(1, c).wait_recv()
            pls[c] = pls[c] + plin[c]

        @pl.when(has_next & has_prev)
        def _():
            wcopy(1, c).start()

        lam = dual[0, :, c]
        new = pls[c]
        base = mv[0, :, c] * (lam - new) + inc[0, :, c]
        pxs[c] = base

        @pl.when((win == 0) & has_next)
        def _():
            gout[c] = base - moved[c, :, pl.ds(PAD, rows), :]
            wcopy(2, c).start()

        wsum[...] = wsum[...] + fold(new * lam)

    order = [(0, c) for c in range(nlev)] + [(1, c) for c in range(nlev)]

    def follow(i):
        @pl.when(is_last)
        def _():
            wcopy(*order[i]).wait_send()
            wcopy(*order[i + 2]).start()

    def diagonal(q):
        for t in range(steps, -1, -1):
            @pl.when((q >= t) & (q - t < nlev))
            def _(t=t):
                if t == 0:
                    adjoint_first(q)
                elif t < steps:
                    adjoint(t - 1, q - t)
                else:
                    adjoint_last(q - t)

        @pl.when(q > steps)
        def _():
            suffix(q - steps - 1)

        for i in range(nlev - 2):
            pl.when(q == 2 * i + 1)(lambda i=i: follow(i))

    for copy in brought:
        copy.wait()
    wsum[...] = zero_tile

    def model(stage):
        now = lax.rem(stage + jnp.where(win == nwin - 1, 1, 0), 2)

        @pl.when(now == 0)
        def _():
            loop(nlev, forward_first)
            follow(nlev - 1)

            def forward_round(s):
                loop(nlev, lambda c: forward(s, c))
                for i in range(nlev - 2):
                    pl.when(s == i)(lambda i=i: follow(nlev + i))

            loop(steps, forward_round)

        @pl.when(now == 1)
        def _():
            loop(nlev + steps + 1, diagonal)
            follow(nlev - 2)

    loop(2, model)

    def observe(c, carry):
        return tuple(
            sum((wgt[o, p, c] * moved[c, p, pl.ds(PAD, rows), :] for p in range(nf)), carry[o])
            for o in range(nobs))

    ends = lax.fori_loop(0, nlev, observe, tuple(jnp.zeros((rows, 128), jnp.float32) for _ in range(nobs)))
    wv0, vv0 = wsum[...], zero_tile
    for o in range(nobs):
        v = obs[0, o]
        pm = (ov[0, o] * v + ends[o]) / ov[0, o]
        oend[o] = pm
        wv0 = wv0 + fold(pm * v)
        vv0 = vv0 + fold(v * v)

    def squares(c, acc):
        return acc + fold(dual[0, :, c] * dual[0, :, c]) + fold(inc[0, :, c] * inc[0, :, c])

    vv = lax.fori_loop(0, nlev, squares, vv0)

    def prefix(c, acc):
        @pl.when(has_prev)
        def _():
            wcopy(2, c).wait_recv()
            pxs[c] = pxs[c] + gin[c]

        @pl.when(has_prev & has_next)
        def _():
            gout[c] = pxs[c] - moved[c, :, pl.ds(PAD, rows), :]
            wcopy(2, c).start()

        return acc + fold(pxs[c] * inc[0, :, c])

    wv = lax.fori_loop(0, nlev, prefix, wv0)

    def total(x):
        return jnp.broadcast_to(jnp.sum(jnp.sum(x, axis=0, keepdims=True), axis=1, keepdims=True), (1, 128))

    def ratio(a, b):
        return jnp.where(b > 0.0, a / jnp.where(b > 0.0, b, 1.0), 0.0)

    wv, vv = total(wv), total(vv)
    h = ratio(wv, vv)

    def residual(c, acc):
        a = pls[c] - h[None] * dual[0, :, c]
        b = pxs[c] - h[None] * inc[0, :, c]
        return acc + fold(a * a) + fold(b * b)

    uu = zero_tile
    for o in range(nobs):
        r = oend[o] - h * obs[0, o]
        uu = uu + fold(r * r)
    uu = total(lax.fori_loop(0, nlev, residual, uu))

    at = 0
    for me, n, partners in rounds:
        red[at + me, 0:1, :] = uu
        red[at + me, 1:2, :] = wv
        red[at + me, 2:3, :] = vv
        swaps = [
            pltpu.make_async_remote_copy(
                src_ref=red.at[at + me], dst_ref=red.at[at + me],
                send_sem=r_send.at[at + j], recv_sem=r_recv.at[at + j],
                device_id=partner, device_id_type=MESH)
            for j, partner in enumerate(partners)]
        for swap in swaps:
            swap.start()
        for swap in swaps:
            swap.wait_recv()
        parts = [tuple(red[at + i, q:q + 1, :] for q in range(3)) for i in range(n)]
        wv = functools.reduce(lambda a, b: a + b, [q[1] for q in parts])
        vv = functools.reduce(lambda a, b: a + b, [q[2] for q in parts])
        h = ratio(wv, vv)
        uu = functools.reduce(
            lambda a, b: a + b, [q[0] + (ratio(q[1], q[2]) - h) * (ratio(q[1], q[2]) - h) * q[2] for q in parts])
        for swap in swaps:
            swap.wait_send()
        at += n

    h = wv / vv
    scale = jnp.sqrt(uu / count + 1e-06)
    inv = 1.0 / scale
    o_co[0] = jnp.sum(jnp.where(lane[0:1] == 0, h, 0.0))
    o_co[1] = jnp.sum(jnp.where(lane[0:1] == 0, scale, 0.0))

    def finish(c):
        o_lam[0, :, c] = (pls[c] - h[None] * dual[0, :, c]) * inv[None]
        o_inc[0, :, c] = (pxs[c] - h[None] * inc[0, :, c]) * inv[None]

    loop(nlev, finish)
    for o in range(nobs):
        o_obs[0, o] = (oend[o] - h * obs[0, o]) * inv

    for kind in range(2):
        pltpu.make_async_remote_copy(
            src_ref=sbuf.at[kind], dst_ref=rbuf.at[kind], send_sem=h_send.at[kind],
            recv_sem=h_recv.at[kind, 0, 0], device_id=to[0], device_id_type=MESH).wait_send()

    @pl.when(is_last)
    def _():
        for i in order[-2:]:
            wcopy(*i).wait_send()

    def settle(c):
        @pl.when(has_prev & has_next)
        def _():
            wcopy(0, c).wait_send()
            wcopy(1, c).wait_send()

        @pl.when(has_next)
        def _():
            wcopy(2, c).wait_send()

    loop(nlev, settle)


def per_device(mesh, dual, obs_dual, increment, trajectory, diffusion, obs_weight, model_var, obs_var):
    nwin, ntx, nty = (mesh.shape[a] for a in ("win", "tx", "ty"))
    _, nf, nlev, rows, cols = dual.shape
    nobs, steps = obs_dual.shape[1], trajectory.shape[1]
    assert cols == 128 and rows % 8 == 0 and steps >= nlev - 2 >= 1 and nf * rows // 4 <= 128 and nf <= 8
    count = (2 * nf * nlev + nobs) * rows * cols * nwin * ntx * nty
    sizes = (nwin, ntx, nty, steps, nf, nlev, rows, nobs, float(count))
    vmem, smem = pl.BlockSpec(memory_space=pltpu.VMEM), pl.BlockSpec(memory_space=pltpu.SMEM)
    chunks = pltpu.VMEM((nlev, nf, rows, cols), jnp.float32)
    messages = pltpu.VMEM((2, steps, nlev, 4, 8, cols), jnp.float32)
    n_red = ntx + nty * nwin
    return pl.pallas_call(
        functools.partial(kernel, sizes),
        out_shape=(
            jax.ShapeDtypeStruct(dual.shape, jnp.float32),
            jax.ShapeDtypeStruct(obs_dual.shape, jnp.float32),
            jax.ShapeDtypeStruct(increment.shape, jnp.float32),
            jax.ShapeDtypeStruct((2,), jnp.float32),
        ),
        in_specs=[pl.BlockSpec(memory_space=pltpu.HBM)] * 8,
        out_specs=(vmem, vmem, vmem, smem),
        scratch_shapes=[
            pltpu.VMEM(dual.shape, jnp.float32), pltpu.VMEM(obs_dual.shape, jnp.float32),
            pltpu.VMEM(increment.shape, jnp.float32), pltpu.VMEM(trajectory.shape, jnp.float32),
            pltpu.VMEM(model_var.shape, jnp.float32), pltpu.VMEM(obs_var.shape, jnp.float32),
            pltpu.SMEM(diffusion.shape, jnp.float32), pltpu.SMEM(obs_weight.shape, jnp.float32),
            pltpu.SemaphoreType.DMA((8,)),
            pltpu.VMEM((2, nlev, nf, rows + 2 * PAD, cols), jnp.float32),
            pltpu.VMEM((2, 5, nlev, nf, rows + 2 * PAD, cols), jnp.float32),
            chunks, chunks, chunks, chunks, chunks, chunks, chunks,
            pltpu.VMEM((nobs, rows, cols), jnp.float32),
            messages, messages,
            pltpu.VMEM((n_red, 8, cols), jnp.float32),
            pltpu.VMEM((8, cols), jnp.float32),
            pltpu.SemaphoreType.DMA((2,)),
            pltpu.SemaphoreType.DMA((2, steps, nlev)),
            pltpu.SemaphoreType.DMA((3, nlev)),
            pltpu.SemaphoreType.DMA((3, nlev)),
            pltpu.SemaphoreType.DMA((n_red,)),
            pltpu.SemaphoreType.DMA((n_red,)),
        ],
        compiler_params=pltpu.CompilerParams(
            collective_id=0, has_side_effects=True, vmem_limit_bytes=60 * 1024 * 1024),
    )(dual, obs_dual, increment, trajectory, model_var, obs_var, diffusion, obs_weight)


def solution(mesh):
    in_specs = (
        P("win", None, None, "ty", "tx"),
        P("win", None, "ty", "tx"),
        P("win", None, None, "ty", "tx"),
        P("win", None, None, None, "ty", "tx"),
        P(),
        P(),
        P("win", None, None, "ty", "tx"),
        P("win", None, "ty", "tx"),
    )
    out_specs = (
        P("win", None, None, "ty", "tx"),
        P("win", None, "ty", "tx"),
        P("win", None, None, "ty", "tx"),
        P(),
    )
    return jax.shard_map(
        functools.partial(per_device, mesh), mesh=mesh, in_specs=in_specs, out_specs=out_specs, check_vma=False
    )
```

```python
import functools
import jax
import jax.numpy as jnp
from jax import lax
from jax.experimental import pallas as pl
from jax.experimental.pallas import tpu as pltpu
from jax.sharding import PartitionSpec as P

MESH = pl.DeviceIdType.MESH
PAD = 8
EAST, WEST, NORTH, SOUTH = range(4)


def kernel(sizes, h_dual, h_obs, h_inc, h_traj, h_mv, h_ov, h_diff, h_wgt,
           o_lam, o_obs, o_inc, o_co,
           dual, obs, inc, traj, mv, ov, diff, wgt, i_sem,
           fld, grd, back, foll, plin, pls, pxs, gin, gout, oend, sbuf, rbuf, red,
           wsum, h_send, h_recv, w_send, w_recv, r_send, r_recv):
    nwin, ntx, nty, steps, nf, nlev, rows, nobs, count = sizes
    groups = rows // 8
    win, tx, ty = lax.axis_index("win"), lax.axis_index("tx"), lax.axis_index("ty")
    has_prev, has_next = win > 0, win < nwin - 1
    right, left = lax.rem(tx + 1, ntx), lax.rem(tx + ntx - 1, ntx)
    lane = lax.broadcasted_iota(jnp.int32, (8, 128), 1)
    is_last = (win == nwin - 1) & has_prev
    rounds = (
        (tx, ntx, [{"tx": lax.rem(tx + j, ntx)} for j in range(1, ntx)]),
        (ty * nwin + win, nty * nwin, [
            {"ty": lax.rem(ty + j // nwin, nty), "win": lax.rem(win + j % nwin, nwin)}
            for j in range(1, nty * nwin)]),
    )

    brought = [
        pltpu.make_async_copy(src, dst, i_sem.at[i])
        for i, (src, dst) in enumerate((
            (h_inc, inc), (h_diff, diff), (h_traj, traj), (h_obs, obs),
            (h_wgt, wgt), (h_dual, dual), (h_mv, mv), (h_ov, ov)))
    ]
    for copy in brought:
        copy.start()

    barrier = pltpu.get_barrier_semaphore()
    for _, _, partners in rounds:
        for partner in partners:
            pl.semaphore_signal(barrier, inc=1, device_id=partner, device_id_type=MESH)

    @pl.when(win == nwin - 1)
    def _():
        foll[...] = jnp.zeros(foll.shape, jnp.float32)
        plin[...] = jnp.zeros(plin.shape, jnp.float32)

    pl.semaphore_wait(barrier, (ntx - 1) + (nty * nwin - 1))

    north_of, south_of = lax.rem(ty + 1, nty), lax.rem(ty + nty - 1, nty)
    to = ({"tx": left}, {"tx": right}, {"ty": south_of}, {"ty": north_of})

    def start_halo(kind, s, c):
        for side in range(4):
            pltpu.make_async_remote_copy(
                src_ref=sbuf.at[kind, s, c, side], dst_ref=rbuf.at[kind, s, c, side],
                send_sem=h_send.at[kind], recv_sem=h_recv.at[kind, s, c],
                device_id=to[side], device_id_type=MESH).start()

    def wait_halo(kind, s, c):
        pltpu.make_async_remote_copy(
            src_ref=sbuf.at[kind, s, c], dst_ref=rbuf.at[kind, s, c],
            send_sem=h_send.at[kind], recv_sem=h_recv.at[kind, s, c],
            device_id=to[0], device_id_type=MESH).wait_recv()

    def edge_rows(kind, s, c):
        north = jnp.where(ty == nty - 1, 0.0, rbuf[kind, s, c, NORTH])
        south = jnp.where(ty == 0, 0.0, rbuf[kind, s, c, SOUTH])
        return north, south

    def wcopy(what, c):
        src, dst, to = (
            (h_dual.at[0, :, c], foll.at[c], win - 1),
            (pls.at[c], plin.at[c], win - 1),
            (gout.at[c], gin.at[c], win + 1),
        )[what]
        return pltpu.make_async_remote_copy(
            src_ref=src, dst_ref=dst, send_sem=w_send.at[what, c], recv_sem=w_recv.at[what, c],
            device_id={"win": to}, device_id_type=MESH)

    @pl.when(has_prev)
    def _():
        for c in range(2):
            wcopy(0, c).start()

    def loop(n, body):
        def step(i, carry):
            body(i)
            return carry
        lax.fori_loop(0, n, step, 0)

    def span(g):
        return pl.ds(8 * g, 8)

    def winds(s, c, g):
        a, b = traj[0, s, 0, c, span(g), :], traj[0, s, 1, c, span(g), :]
        pa, pb = jnp.maximum(a, 0.0), jnp.maximum(b, 0.0)
        ma, mb = pa - a, pb - b
        return pa, ma, pb, mb, 1.0 - ((pa + ma) + (pb + mb))

    pair = lane >> 1

    def into(acc, value, k):
        return jnp.where(pair == k, pltpu.roll(value, 2 * k + 1, 1), acc)

    def edge_columns(kind, s, c):
        return jnp.where(
            lane == 2 * pair, pltpu.roll(rbuf[kind, s, c, EAST], 127, 1), pltpu.roll(rbuf[kind, s, c, WEST], 1, 1))

    def shifted(for_east, for_west, columns, k):
        edge = pltpu.roll(columns, (127 - 2 * k) % 128, 1)
        east = jnp.where(lane == 127, edge, pltpu.roll(for_east, 127, 1))
        west = jnp.where(lane == 0, edge, pltpu.roll(for_west, 1, 1))
        return east, west

    zero_tile = jnp.zeros((8, 128), jnp.float32)

    def forward_first(c):
        packed = zero_tile
        for p in range(nf):
            for g in range(groups):
                value = inc[0, p, c, span(g), :]
                fld[0, c, p, pl.ds(PAD + 8 * g, 8), :] = value
                packed = into(packed, value, p * groups + g)
            sbuf[0, 0, c, NORTH, p, :] = inc[0, p, c, 0, :]
            sbuf[0, 0, c, SOUTH, p, :] = inc[0, p, c, rows - 1, :]
        sbuf[0, 0, c, EAST] = packed
        sbuf[0, 0, c, WEST] = packed
        start_halo(0, 0, c)


    def forward(s, c):
        wait_halo(0, s, c)
        now, later = lax.rem(s, 2), lax.rem(s + 1, 2)
        north_row, south_row = edge_rows(0, s, c)
        for p in range(nf):
            fld[now, c, p, PAD - 1, :] = south_row[p]
            fld[now, c, p, PAD + rows, :] = north_row[p]
        columns = edge_columns(0, s, c)
        packed = zero_tile
        ks = [diff[p, c] for p in range(nf)]
        after = jnp.minimum(s + 1, steps - 1)
        fresh = []
        for g in range(groups):
            pa, ma, pb, mb, d = winds(s, c, g)
            for p in range(nf):
                k = ks[p]
                x = fld[now, c, p, pl.ds(PAD + 8 * g, 8), :]
                north = fld[now, c, p, pl.ds(PAD + 8 * g + 1, 8), :]
                south = fld[now, c, p, pl.ds(PAD + 8 * g - 1, 8), :]
                place = p * groups + g
                east, west = shifted(x, x, columns, place)
                new = (d - 4.0 * k) * x + (pa + k) * west + (ma + k) * east + (pb + k) * south + (mb + k) * north
                fresh.append((p, g, new))
                packed = into(packed, new, place)
        for p, g, new in fresh:
            fld[later, c, p, pl.ds(PAD + 8 * g, 8), :] = new

        @pl.when(s < steps - 1)
        def _():
            for p in range(nf):
                sbuf[0, after, c, NORTH, p, :] = fld[later, c, p, PAD, :]
                sbuf[0, after, c, SOUTH, p, :] = fld[later, c, p, PAD + rows - 1, :]
            sbuf[0, after, c, EAST] = packed
            sbuf[0, after, c, WEST] = packed
            start_halo(0, after, c)

    moved = fld.at[steps % 2]

    def products(y, w, k, slot, c, p, g):
        pa, ma, pb, mb, d = w
        g_east, g_west = (pa + k) * y, (ma + k) * y
        here = pl.ds(PAD + 8 * g, 8)
        grd[slot, 0, c, p, here, :] = g_east
        grd[slot, 1, c, p, here, :] = g_west
        grd[slot, 2, c, p, here, :] = (pb + k) * y
        grd[slot, 3, c, p, here, :] = (mb + k) * y
        grd[slot, 4, c, p, here, :] = (d - 4.0 * k) * y
        return jnp.where(lane == 0, g_east, g_west)

    def ship(t, slot, c, packed):
        for p in range(nf):
            sbuf[1, t, c, NORTH, p, :] = grd[slot, 2, c, p, PAD, :]
            sbuf[1, t, c, SOUTH, p, :] = grd[slot, 3, c, p, PAD + rows - 1, :]
        sbuf[1, t, c, EAST] = packed
        sbuf[1, t, c, WEST] = packed
        start_halo(1, t, c)

    def adjoint_first(c):
        @pl.when(has_next)
        def _():
            wcopy(0, c).wait_recv()

        packed = zero_tile
        ks = [diff[p, c] for p in range(nf)]
        ws = [[wgt[o, p, c] for o in range(nobs)] for p in range(nf)]
        start = {}
        for g in range(groups):
            observed = [obs[0, o, span(g), :] for o in range(nobs)]
            for p in range(nf):
                y = -foll[c, p, span(g), :]
                for o in range(nobs):
                    y = y + ws[p][o] * observed[o]
                start[p, g] = y
        for g in range(groups):
            w = winds(steps - 1, c, g)
            for p in range(nf):
                packed = into(packed, products(start[p, g], w, ks[p], 0, c, p, g), p * groups + g)
        ship(0, 0, c, packed)


    def gathered(slot, c, p, g, columns):
        here = pl.ds(PAD + 8 * g, 8)
        east, west = shifted(grd[slot, 0, c, p, here, :], grd[slot, 1, c, p, here, :], columns, p * groups + g)
        north = grd[slot, 2, c, p, pl.ds(PAD + 8 * g + 1, 8), :]
        south = grd[slot, 3, c, p, pl.ds(PAD + 8 * g - 1, 8), :]
        return grd[slot, 4, c, p, here, :] + ((east + west) + (north + south))

    def receive(t, slot, c):
        wait_halo(1, t, c)
        north_row, south_row = edge_rows(1, t, c)
        for p in range(nf):
            grd[slot, 2, c, p, PAD + rows, :] = north_row[p]
            grd[slot, 3, c, p, PAD - 1, :] = south_row[p]
        return edge_columns(1, t, c)

    def adjoint(t, c):
        slot, other = lax.rem(t, 2), lax.rem(t + 1, 2)
        columns = receive(t, slot, c)
        packed = zero_tile
        ks = [diff[p, c] for p in range(nf)]
        start = {
            (p, g): gathered(slot, c, p, g, columns)
            for g in range(groups) for p in range(nf)}
        for g in range(groups):
            w = winds(steps - 2 - t, c, g)
            for p in range(nf):
                packed = into(packed, products(start[p, g], w, ks[p], other, c, p, g), p * groups + g)
        ship(t + 1, other, c, packed)


    def adjoint_last(c):
        slot = (steps - 1) % 2
        columns = receive(steps - 1, slot, c)
        done = {
            (p, g): gathered(slot, c, p, g, columns)
            for g in range(groups) for p in range(nf)}
        for (p, g), y in done.items():
            back[c, p, span(g), :] = y
        pls[c] = dual[0, :, c] + back[c]

        @pl.when(is_last)
        def _():
            wcopy(1, c).start()

    def fold(x):
        return jnp.sum(x.reshape(-1, 8, 128), axis=0)

    def suffix(c):
        @pl.when(has_next)
        def _():
            wcopy(1, c).wait_recv()
            pls[c] = pls[c] + plin[c]

        @pl.when(has_next & has_prev)
        def _():
            wcopy(1, c).start()

        lam = dual[0, :, c]
        new = pls[c]
        base = mv[0, :, c] * (lam - new) + inc[0, :, c]
        pxs[c] = base

        @pl.when((win == 0) & has_next)
        def _():
            gout[c] = base - moved[c, :, pl.ds(PAD, rows), :]
            wcopy(2, c).start()

        wsum[...] = wsum[...] + fold(new * lam)

    def follow(c):
        @pl.when(has_prev)
        def _():
            wcopy(0, c).wait_send()
            wcopy(0, c + 2).start()

    def slot_of_work(q):
        @pl.when(q == 0)
        def _():
            loop(nlev, forward_first)

        @pl.when((q >= 1) & (q <= steps))
        def _():
            loop(nlev, lambda c: forward(q - 1, c))

        for t in range(steps, -1, -1):
            @pl.when((q >= t) & (q - t < nlev))
            def _(t=t):
                if t == 0:
                    adjoint_first(q)
                elif t < steps:
                    adjoint(t - 1, q - t)
                else:
                    adjoint_last(q - t)

        @pl.when(q > steps)
        def _():
            suffix(q - steps - 1)

        for i in range(nlev - 2):
            pl.when(q == i)(lambda i=i: follow(i))

    for copy in brought:
        copy.wait()
    wsum[...] = zero_tile

    loop(nlev + steps + 1, slot_of_work)

    def observe(c, carry):
        return tuple(
            sum((wgt[o, p, c] * moved[c, p, pl.ds(PAD, rows), :] for p in range(nf)), carry[o])
            for o in range(nobs))

    ends = lax.fori_loop(0, nlev, observe, tuple(jnp.zeros((rows, 128), jnp.float32) for _ in range(nobs)))
    wv0, vv0 = wsum[...], zero_tile
    for o in range(nobs):
        v = obs[0, o]
        pm = (ov[0, o] * v + ends[o]) / ov[0, o]
        oend[o] = pm
        wv0 = wv0 + fold(pm * v)
        vv0 = vv0 + fold(v * v)

    def squares(c, acc):
        return acc + fold(dual[0, :, c] * dual[0, :, c]) + fold(inc[0, :, c] * inc[0, :, c])

    vv = lax.fori_loop(0, nlev, squares, vv0)

    def prefix(c, acc):
        @pl.when(has_prev)
        def _():
            wcopy(2, c).wait_recv()
            pxs[c] = pxs[c] + gin[c]

        @pl.when(has_prev & has_next)
        def _():
            gout[c] = pxs[c] - moved[c, :, pl.ds(PAD, rows), :]
            wcopy(2, c).start()

        return acc + fold(pxs[c] * inc[0, :, c])

    wv = lax.fori_loop(0, nlev, prefix, wv0)

    def total(x):
        return jnp.broadcast_to(jnp.sum(jnp.sum(x, axis=0, keepdims=True), axis=1, keepdims=True), (1, 128))

    def ratio(a, b):
        return jnp.where(b > 0.0, a / jnp.where(b > 0.0, b, 1.0), 0.0)

    wv, vv = total(wv), total(vv)
    h = ratio(wv, vv)

    def residual(c, acc):
        a = pls[c] - h[None] * dual[0, :, c]
        b = pxs[c] - h[None] * inc[0, :, c]
        return acc + fold(a * a) + fold(b * b)

    uu = zero_tile
    for o in range(nobs):
        r = oend[o] - h * obs[0, o]
        uu = uu + fold(r * r)
    uu = total(lax.fori_loop(0, nlev, residual, uu))

    at = 0
    for me, n, partners in rounds:
        red[at + me, 0:1, :] = uu
        red[at + me, 1:2, :] = wv
        red[at + me, 2:3, :] = vv
        swaps = [
            pltpu.make_async_remote_copy(
                src_ref=red.at[at + me], dst_ref=red.at[at + me],
                send_sem=r_send.at[at + j], recv_sem=r_recv.at[at + j],
                device_id=partner, device_id_type=MESH)
            for j, partner in enumerate(partners)]
        for swap in swaps:
            swap.start()
        for swap in swaps:
            swap.wait_recv()
        parts = [tuple(red[at + i, q:q + 1, :] for q in range(3)) for i in range(n)]
        wv = functools.reduce(lambda a, b: a + b, [q[1] for q in parts])
        vv = functools.reduce(lambda a, b: a + b, [q[2] for q in parts])
        h = ratio(wv, vv)
        uu = functools.reduce(
            lambda a, b: a + b, [q[0] + (ratio(q[1], q[2]) - h) * (ratio(q[1], q[2]) - h) * q[2] for q in parts])
        for swap in swaps:
            swap.wait_send()
        at += n

    h = wv / vv
    scale = jnp.sqrt(uu / count + 1e-06)
    inv = 1.0 / scale
    o_co[0] = jnp.sum(jnp.where(lane[0:1] == 0, h, 0.0))
    o_co[1] = jnp.sum(jnp.where(lane[0:1] == 0, scale, 0.0))

    def finish(c):
        o_lam[0, :, c] = (pls[c] - h[None] * dual[0, :, c]) * inv[None]
        o_inc[0, :, c] = (pxs[c] - h[None] * inc[0, :, c]) * inv[None]

    loop(nlev, finish)
    for o in range(nobs):
        o_obs[0, o] = (oend[o] - h * obs[0, o]) * inv

    for kind in range(2):
        pltpu.make_async_remote_copy(
            src_ref=sbuf.at[kind], dst_ref=rbuf.at[kind], send_sem=h_send.at[kind],
            recv_sem=h_recv.at[kind, 0, 0], device_id=to[0], device_id_type=MESH).wait_send()

    def settle(c):
        @pl.when(has_prev)
        def _():
            wcopy(1, c).wait_send()

        @pl.when(has_prev & (c >= nlev - 2))
        def _():
            wcopy(0, c).wait_send()

        @pl.when(has_next)
        def _():
            wcopy(2, c).wait_send()

    loop(nlev, settle)


def per_device(mesh, dual, obs_dual, increment, trajectory, diffusion, obs_weight, model_var, obs_var):
    nwin, ntx, nty = (mesh.shape[a] for a in ("win", "tx", "ty"))
    _, nf, nlev, rows, cols = dual.shape
    nobs, steps = obs_dual.shape[1], trajectory.shape[1]
    assert cols == 128 and rows % 8 == 0 and nlev >= 2 and nf * rows // 4 <= 128 and nf <= 8
    count = (2 * nf * nlev + nobs) * rows * cols * nwin * ntx * nty
    sizes = (nwin, ntx, nty, steps, nf, nlev, rows, nobs, float(count))
    vmem, smem = pl.BlockSpec(memory_space=pltpu.VMEM), pl.BlockSpec(memory_space=pltpu.SMEM)
    chunks = pltpu.VMEM((nlev, nf, rows, cols), jnp.float32)
    messages = pltpu.VMEM((2, steps, nlev, 4, 8, cols), jnp.float32)
    n_red = ntx + nty * nwin
    return pl.pallas_call(
        functools.partial(kernel, sizes),
        out_shape=(
            jax.ShapeDtypeStruct(dual.shape, jnp.float32),
            jax.ShapeDtypeStruct(obs_dual.shape, jnp.float32),
            jax.ShapeDtypeStruct(increment.shape, jnp.float32),
            jax.ShapeDtypeStruct((2,), jnp.float32),
        ),
        in_specs=[pl.BlockSpec(memory_space=pltpu.HBM)] * 8,
        out_specs=(vmem, vmem, vmem, smem),
        scratch_shapes=[
            pltpu.VMEM(dual.shape, jnp.float32), pltpu.VMEM(obs_dual.shape, jnp.float32),
            pltpu.VMEM(increment.shape, jnp.float32), pltpu.VMEM(trajectory.shape, jnp.float32),
            pltpu.VMEM(model_var.shape, jnp.float32), pltpu.VMEM(obs_var.shape, jnp.float32),
            pltpu.SMEM(diffusion.shape, jnp.float32), pltpu.SMEM(obs_weight.shape, jnp.float32),
            pltpu.SemaphoreType.DMA((8,)),
            pltpu.VMEM((2, nlev, nf, rows + 2 * PAD, cols), jnp.float32),
            pltpu.VMEM((2, 5, nlev, nf, rows + 2 * PAD, cols), jnp.float32),
            chunks, chunks, chunks, chunks, chunks, chunks, chunks,
            pltpu.VMEM((nobs, rows, cols), jnp.float32),
            messages, messages,
            pltpu.VMEM((n_red, 8, cols), jnp.float32),
            pltpu.VMEM((8, cols), jnp.float32),
            pltpu.SemaphoreType.DMA((2,)),
            pltpu.SemaphoreType.DMA((2, steps, nlev)),
            pltpu.SemaphoreType.DMA((3, nlev)),
            pltpu.SemaphoreType.DMA((3, nlev)),
            pltpu.SemaphoreType.DMA((n_red,)),
            pltpu.SemaphoreType.DMA((n_red,)),
        ],
        compiler_params=pltpu.CompilerParams(
            collective_id=0, has_side_effects=True, vmem_limit_bytes=60 * 1024 * 1024),
    )(dual, obs_dual, increment, trajectory, model_var, obs_var, diffusion, obs_weight)


def solution(mesh):
    in_specs = (
        P("win", None, None, "ty", "tx"),
        P("win", None, "ty", "tx"),
        P("win", None, None, "ty", "tx"),
        P("win", None, None, None, "ty", "tx"),
        P(),
        P(),
        P("win", None, None, "ty", "tx"),
        P("win", None, "ty", "tx"),
    )
    out_specs = (
        P("win", None, None, "ty", "tx"),
        P("win", None, "ty", "tx"),
        P("win", None, None, "ty", "tx"),
        P(),
    )
    return jax.shard_map(
        functools.partial(per_device, mesh), mesh=mesh, in_specs=in_specs, out_specs=out_specs, check_vma=False
    )
```

```python
import functools
import jax
import jax.numpy as jnp
from jax import lax
from jax.experimental import pallas as pl
from jax.experimental.pallas import tpu as pltpu
from jax.sharding import PartitionSpec as P

MESH = pl.DeviceIdType.MESH
PAD = 8
EAST, WEST, NORTH, SOUTH = range(4)


def kernel(sizes, h_dual, h_obs, h_inc, h_traj, h_mv, h_ov, h_diff, h_wgt,
           o_lam, o_obs, o_inc, o_co,
           dual, obs, inc, traj, mv, ov, diff, wgt, i_sem,
           fld, grd, back, foll, plin, pls, pxs, gin, gout, oend, sbuf, rbuf, red,
           wsum, h_send, h_recv, w_send, w_recv, r_send, r_recv):
    nwin, ntx, nty, steps, nf, nlev, rows, nobs, count = sizes
    groups = rows // 8
    win, tx, ty = lax.axis_index("win"), lax.axis_index("tx"), lax.axis_index("ty")
    has_prev, has_next = win > 0, win < nwin - 1
    right, left = lax.rem(tx + 1, ntx), lax.rem(tx + ntx - 1, ntx)
    lane = lax.broadcasted_iota(jnp.int32, (8, 128), 1)
    is_last = (win == nwin - 1) & has_prev
    rounds = (
        (tx, ntx, [{"tx": lax.rem(tx + j, ntx)} for j in range(1, ntx)]),
        (ty * nwin + win, nty * nwin, [
            {"ty": lax.rem(ty + j // nwin, nty), "win": lax.rem(win + j % nwin, nwin)}
            for j in range(1, nty * nwin)]),
    )

    brought = [
        pltpu.make_async_copy(src, dst, i_sem.at[i])
        for i, (src, dst) in enumerate((
            (h_inc, inc), (h_diff, diff), (h_traj, traj), (h_obs, obs),
            (h_wgt, wgt), (h_dual, dual), (h_mv, mv), (h_ov, ov)))
    ]
    for copy in brought:
        copy.start()

    barrier = pltpu.get_barrier_semaphore()
    for _, _, partners in rounds:
        for partner in partners:
            pl.semaphore_signal(barrier, inc=1, device_id=partner, device_id_type=MESH)

    @pl.when(win == nwin - 1)
    def _():
        foll[...] = jnp.zeros(foll.shape, jnp.float32)
        plin[...] = jnp.zeros(plin.shape, jnp.float32)

    pl.semaphore_wait(barrier, (ntx - 1) + (nty * nwin - 1))

    north_of, south_of = lax.rem(ty + 1, nty), lax.rem(ty + nty - 1, nty)
    to = ({"tx": left}, {"tx": right}, {"ty": south_of}, {"ty": north_of})

    def start_halo(kind, s, c):
        for side in range(4):
            pltpu.make_async_remote_copy(
                src_ref=sbuf.at[kind, s, c, side], dst_ref=rbuf.at[kind, s, c, side],
                send_sem=h_send.at[kind], recv_sem=h_recv.at[kind, s, c],
                device_id=to[side], device_id_type=MESH).start()

    def wait_halo(kind, s, c):
        pltpu.make_async_remote_copy(
            src_ref=sbuf.at[kind, s, c], dst_ref=rbuf.at[kind, s, c],
            send_sem=h_send.at[kind], recv_sem=h_recv.at[kind, s, c],
            device_id=to[0], device_id_type=MESH).wait_recv()

    def edge_rows(kind, s, c):
        north = jnp.where(ty == nty - 1, 0.0, rbuf[kind, s, c, NORTH])
        south = jnp.where(ty == 0, 0.0, rbuf[kind, s, c, SOUTH])
        return north, south

    def wcopy(what, c):
        src, dst, to = (
            (h_dual.at[0, :, c], foll.at[c], win - 1),
            (pls.at[c], plin.at[c], win - 1),
            (gout.at[c], gin.at[c], win + 1),
        )[what]
        return pltpu.make_async_remote_copy(
            src_ref=src, dst_ref=dst, send_sem=w_send.at[what, c], recv_sem=w_recv.at[what, c],
            device_id={"win": to}, device_id_type=MESH)

    @pl.when(has_prev)
    def _():
        for c in range(2):
            wcopy(0, c).start()

    def loop(n, body):
        def step(i, carry):
            body(i)
            return carry
        lax.fori_loop(0, n, step, 0)

    def span(g):
        return pl.ds(8 * g, 8)

    def winds(s, c, g):
        a, b = traj[0, s, 0, c, span(g), :], traj[0, s, 1, c, span(g), :]
        pa, pb = jnp.maximum(a, 0.0), jnp.maximum(b, 0.0)
        ma, mb = pa - a, pb - b
        return pa, ma, pb, mb, 1.0 - ((pa + ma) + (pb + mb))

    pair = lane >> 1

    def into(acc, value, k):
        return jnp.where(pair == k, pltpu.roll(value, 2 * k + 1, 1), acc)

    def edge_columns(kind, s, c):
        return jnp.where(
            lane == 2 * pair, pltpu.roll(rbuf[kind, s, c, EAST], 127, 1), pltpu.roll(rbuf[kind, s, c, WEST], 1, 1))

    def shifted(for_east, for_west, columns, k):
        edge = pltpu.roll(columns, (127 - 2 * k) % 128, 1)
        east = jnp.where(lane == 127, edge, pltpu.roll(for_east, 127, 1))
        west = jnp.where(lane == 0, edge, pltpu.roll(for_west, 1, 1))
        return east, west

    zero_tile = jnp.zeros((8, 128), jnp.float32)

    def forward_first(c):
        packed = zero_tile
        for p in range(nf):
            for g in range(groups):
                value = inc[0, p, c, span(g), :]
                fld[0, c, p, pl.ds(PAD + 8 * g, 8), :] = value
                packed = into(packed, value, p * groups + g)
            sbuf[0, 0, c, NORTH, p, :] = inc[0, p, c, 0, :]
            sbuf[0, 0, c, SOUTH, p, :] = inc[0, p, c, rows - 1, :]
        sbuf[0, 0, c, EAST] = packed
        sbuf[0, 0, c, WEST] = packed
        start_halo(0, 0, c)


    def forward(s, c):
        wait_halo(0, s, c)
        now, later = lax.rem(s, 2), lax.rem(s + 1, 2)
        north_row, south_row = edge_rows(0, s, c)
        for p in range(nf):
            fld[now, c, p, PAD - 1, :] = south_row[p]
            fld[now, c, p, PAD + rows, :] = north_row[p]
        columns = edge_columns(0, s, c)
        packed = zero_tile
        ks = [diff[p, c] for p in range(nf)]
        after = jnp.minimum(s + 1, steps - 1)
        fresh = []
        for g in range(groups):
            pa, ma, pb, mb, d = winds(s, c, g)
            for p in range(nf):
                k = ks[p]
                x = fld[now, c, p, pl.ds(PAD + 8 * g, 8), :]
                north = fld[now, c, p, pl.ds(PAD + 8 * g + 1, 8), :]
                south = fld[now, c, p, pl.ds(PAD + 8 * g - 1, 8), :]
                place = p * groups + g
                east, west = shifted(x, x, columns, place)
                new = (d - 4.0 * k) * x + (pa + k) * west + (ma + k) * east + (pb + k) * south + (mb + k) * north
                fresh.append((p, g, new))
                packed = into(packed, new, place)
        for p, g, new in fresh:
            fld[later, c, p, pl.ds(PAD + 8 * g, 8), :] = new

        @pl.when(s < steps - 1)
        def _():
            for p in range(nf):
                sbuf[0, after, c, NORTH, p, :] = fld[later, c, p, PAD, :]
                sbuf[0, after, c, SOUTH, p, :] = fld[later, c, p, PAD + rows - 1, :]
            sbuf[0, after, c, EAST] = packed
            sbuf[0, after, c, WEST] = packed
            start_halo(0, after, c)

    moved = fld.at[steps % 2]

    def products(y, w, k, slot, c, p, g):
        pa, ma, pb, mb, d = w
        g_east, g_west = (pa + k) * y, (ma + k) * y
        here = pl.ds(PAD + 8 * g, 8)
        grd[slot, 0, c, p, here, :] = g_east
        grd[slot, 1, c, p, here, :] = g_west
        grd[slot, 2, c, p, here, :] = (pb + k) * y
        grd[slot, 3, c, p, here, :] = (mb + k) * y
        grd[slot, 4, c, p, here, :] = (d - 4.0 * k) * y
        return jnp.where(lane == 0, g_east, g_west)

    def ship(t, slot, c, packed):
        for p in range(nf):
            sbuf[1, t, c, NORTH, p, :] = grd[slot, 2, c, p, PAD, :]
            sbuf[1, t, c, SOUTH, p, :] = grd[slot, 3, c, p, PAD + rows - 1, :]
        sbuf[1, t, c, EAST] = packed
        sbuf[1, t, c, WEST] = packed
        start_halo(1, t, c)

    def adjoint_first(c):
        @pl.when(has_next)
        def _():
            wcopy(0, c).wait_recv()

        packed = zero_tile
        ks = [diff[p, c] for p in range(nf)]
        ws = [[wgt[o, p, c] for o in range(nobs)] for p in range(nf)]
        start = {}
        for g in range(groups):
            observed = [obs[0, o, span(g), :] for o in range(nobs)]
            for p in range(nf):
                y = -foll[c, p, span(g), :]
                for o in range(nobs):
                    y = y + ws[p][o] * observed[o]
                start[p, g] = y
        for g in range(groups):
            w = winds(steps - 1, c, g)
            for p in range(nf):
                packed = into(packed, products(start[p, g], w, ks[p], 0, c, p, g), p * groups + g)
        ship(0, 0, c, packed)


    def gathered(slot, c, p, g, columns):
        here = pl.ds(PAD + 8 * g, 8)
        east, west = shifted(grd[slot, 0, c, p, here, :], grd[slot, 1, c, p, here, :], columns, p * groups + g)
        north = grd[slot, 2, c, p, pl.ds(PAD + 8 * g + 1, 8), :]
        south = grd[slot, 3, c, p, pl.ds(PAD + 8 * g - 1, 8), :]
        return grd[slot, 4, c, p, here, :] + ((east + west) + (north + south))

    def receive(t, slot, c):
        wait_halo(1, t, c)
        north_row, south_row = edge_rows(1, t, c)
        for p in range(nf):
            grd[slot, 2, c, p, PAD + rows, :] = north_row[p]
            grd[slot, 3, c, p, PAD - 1, :] = south_row[p]
        return edge_columns(1, t, c)

    def adjoint(t, c):
        slot, other = lax.rem(t, 2), lax.rem(t + 1, 2)
        columns = receive(t, slot, c)
        packed = zero_tile
        ks = [diff[p, c] for p in range(nf)]
        start = {
            (p, g): gathered(slot, c, p, g, columns)
            for g in range(groups) for p in range(nf)}
        for g in range(groups):
            w = winds(steps - 2 - t, c, g)
            for p in range(nf):
                packed = into(packed, products(start[p, g], w, ks[p], other, c, p, g), p * groups + g)
        ship(t + 1, other, c, packed)


    def adjoint_last(c):
        slot = (steps - 1) % 2
        columns = receive(steps - 1, slot, c)
        done = {
            (p, g): gathered(slot, c, p, g, columns)
            for g in range(groups) for p in range(nf)}
        for (p, g), y in done.items():
            back[c, p, span(g), :] = y
        pls[c] = dual[0, :, c] + back[c]

        @pl.when(is_last)
        def _():
            wcopy(1, c).start()

    def fold(x):
        return jnp.sum(x.reshape(-1, 8, 128), axis=0)

    def suffix(c):
        @pl.when(has_next)
        def _():
            wcopy(1, c).wait_recv()
            pls[c] = pls[c] + plin[c]

        @pl.when(has_next & has_prev)
        def _():
            wcopy(1, c).start()

        lam = dual[0, :, c]
        new = pls[c]
        base = mv[0, :, c] * (lam - new) + inc[0, :, c]
        pxs[c] = base

        @pl.when((win == 0) & has_next)
        def _():
            gout[c] = base - moved[c, :, pl.ds(PAD, rows), :]
            wcopy(2, c).start()

        wsum[...] = wsum[...] + fold(new * lam)

    def begun(slot, body):
        def one(i):
            c = 2 * slot - 1 + i
            pl.when((c >= 0) & (c < nlev))(lambda: body(c))
        loop(2, one)

    def slot_of_work(q):
        @pl.when(q == 0)
        def _():
            loop(nlev, forward_first)

        @pl.when((q >= 1) & (q <= steps))
        def _():
            loop(nlev, lambda c: forward(q - 1, c))

        @pl.when(has_prev & (q + 2 < nlev))
        def _():
            wcopy(0, q + 2).start()

        for t in range(steps, -1, -1):
            begun(q - t, adjoint_first if t == 0 else adjoint_last if t == steps else functools.partial(adjoint, t - 1))
        begun(q - steps - 1, suffix)

    for copy in brought:
        copy.wait()
    wsum[...] = zero_tile

    loop(nlev // 2 + steps + 2, slot_of_work)

    def observe(c, carry):
        return tuple(
            sum((wgt[o, p, c] * moved[c, p, pl.ds(PAD, rows), :] for p in range(nf)), carry[o])
            for o in range(nobs))

    ends = lax.fori_loop(0, nlev, observe, tuple(jnp.zeros((rows, 128), jnp.float32) for _ in range(nobs)))
    wv0, vv0 = wsum[...], zero_tile
    for o in range(nobs):
        v = obs[0, o]
        pm = (ov[0, o] * v + ends[o]) / ov[0, o]
        oend[o] = pm
        wv0 = wv0 + fold(pm * v)
        vv0 = vv0 + fold(v * v)

    def squares(c, acc):
        return acc + fold(dual[0, :, c] * dual[0, :, c]) + fold(inc[0, :, c] * inc[0, :, c])

    vv = lax.fori_loop(0, nlev, squares, vv0)

    def prefix(c, acc):
        @pl.when(has_prev)
        def _():
            wcopy(2, c).wait_recv()
            pxs[c] = pxs[c] + gin[c]

        @pl.when(has_prev & has_next)
        def _():
            gout[c] = pxs[c] - moved[c, :, pl.ds(PAD, rows), :]
            wcopy(2, c).start()

        return acc + fold(pxs[c] * inc[0, :, c])

    wv = lax.fori_loop(0, nlev, prefix, wv0)

    def total(x):
        return jnp.broadcast_to(jnp.sum(jnp.sum(x, axis=0, keepdims=True), axis=1, keepdims=True), (1, 128))

    def ratio(a, b):
        return jnp.where(b > 0.0, a / jnp.where(b > 0.0, b, 1.0), 0.0)

    wv, vv = total(wv), total(vv)
    h = ratio(wv, vv)

    def residual(c, acc):
        a = pls[c] - h[None] * dual[0, :, c]
        b = pxs[c] - h[None] * inc[0, :, c]
        return acc + fold(a * a) + fold(b * b)

    uu = zero_tile
    for o in range(nobs):
        r = oend[o] - h * obs[0, o]
        uu = uu + fold(r * r)
    uu = total(lax.fori_loop(0, nlev, residual, uu))

    at = 0
    for me, n, partners in rounds:
        red[at + me, 0:1, :] = uu
        red[at + me, 1:2, :] = wv
        red[at + me, 2:3, :] = vv
        swaps = [
            pltpu.make_async_remote_copy(
                src_ref=red.at[at + me], dst_ref=red.at[at + me],
                send_sem=r_send.at[at + j], recv_sem=r_recv.at[at + j],
                device_id=partner, device_id_type=MESH)
            for j, partner in enumerate(partners)]
        for swap in swaps:
            swap.start()
        for swap in swaps:
            swap.wait_recv()
        parts = [tuple(red[at + i, q:q + 1, :] for q in range(3)) for i in range(n)]
        wv = functools.reduce(lambda a, b: a + b, [q[1] for q in parts])
        vv = functools.reduce(lambda a, b: a + b, [q[2] for q in parts])
        h = ratio(wv, vv)
        uu = functools.reduce(
            lambda a, b: a + b, [q[0] + (ratio(q[1], q[2]) - h) * (ratio(q[1], q[2]) - h) * q[2] for q in parts])
        for swap in swaps:
            swap.wait_send()
        at += n

    h = wv / vv
    scale = jnp.sqrt(uu / count + 1e-06)
    inv = 1.0 / scale
    o_co[0] = jnp.sum(jnp.where(lane[0:1] == 0, h, 0.0))
    o_co[1] = jnp.sum(jnp.where(lane[0:1] == 0, scale, 0.0))

    def finish(c):
        o_lam[0, :, c] = (pls[c] - h[None] * dual[0, :, c]) * inv[None]
        o_inc[0, :, c] = (pxs[c] - h[None] * inc[0, :, c]) * inv[None]

    loop(nlev, finish)
    for o in range(nobs):
        o_obs[0, o] = (oend[o] - h * obs[0, o]) * inv

    for kind in range(2):
        pltpu.make_async_remote_copy(
            src_ref=sbuf.at[kind], dst_ref=rbuf.at[kind], send_sem=h_send.at[kind],
            recv_sem=h_recv.at[kind, 0, 0], device_id=to[0], device_id_type=MESH).wait_send()

    def settle(c):
        @pl.when(has_prev)
        def _():
            wcopy(0, c).wait_send()
            wcopy(1, c).wait_send()

        @pl.when(has_next)
        def _():
            wcopy(2, c).wait_send()

    loop(nlev, settle)


def per_device(mesh, dual, obs_dual, increment, trajectory, diffusion, obs_weight, model_var, obs_var):
    nwin, ntx, nty = (mesh.shape[a] for a in ("win", "tx", "ty"))
    _, nf, nlev, rows, cols = dual.shape
    nobs, steps = obs_dual.shape[1], trajectory.shape[1]
    assert cols == 128 and rows % 8 == 0 and nlev >= 2 and nf * rows // 4 <= 128 and nf <= 8
    count = (2 * nf * nlev + nobs) * rows * cols * nwin * ntx * nty
    sizes = (nwin, ntx, nty, steps, nf, nlev, rows, nobs, float(count))
    vmem, smem = pl.BlockSpec(memory_space=pltpu.VMEM), pl.BlockSpec(memory_space=pltpu.SMEM)
    chunks = pltpu.VMEM((nlev, nf, rows, cols), jnp.float32)
    messages = pltpu.VMEM((2, steps, nlev, 4, 8, cols), jnp.float32)
    n_red = ntx + nty * nwin
    return pl.pallas_call(
        functools.partial(kernel, sizes),
        out_shape=(
            jax.ShapeDtypeStruct(dual.shape, jnp.float32),
            jax.ShapeDtypeStruct(obs_dual.shape, jnp.float32),
            jax.ShapeDtypeStruct(increment.shape, jnp.float32),
            jax.ShapeDtypeStruct((2,), jnp.float32),
        ),
        in_specs=[pl.BlockSpec(memory_space=pltpu.HBM)] * 8,
        out_specs=(vmem, vmem, vmem, smem),
        scratch_shapes=[
            pltpu.VMEM(dual.shape, jnp.float32), pltpu.VMEM(obs_dual.shape, jnp.float32),
            pltpu.VMEM(increment.shape, jnp.float32), pltpu.VMEM(trajectory.shape, jnp.float32),
            pltpu.VMEM(model_var.shape, jnp.float32), pltpu.VMEM(obs_var.shape, jnp.float32),
            pltpu.SMEM(diffusion.shape, jnp.float32), pltpu.SMEM(obs_weight.shape, jnp.float32),
            pltpu.SemaphoreType.DMA((8,)),
            pltpu.VMEM((2, nlev, nf, rows + 2 * PAD, cols), jnp.float32),
            pltpu.VMEM((2, 5, nlev, nf, rows + 2 * PAD, cols), jnp.float32),
            chunks, chunks, chunks, chunks, chunks, chunks, chunks,
            pltpu.VMEM((nobs, rows, cols), jnp.float32),
            messages, messages,
            pltpu.VMEM((n_red, 8, cols), jnp.float32),
            pltpu.VMEM((8, cols), jnp.float32),
            pltpu.SemaphoreType.DMA((2,)),
            pltpu.SemaphoreType.DMA((2, steps, nlev)),
            pltpu.SemaphoreType.DMA((3, nlev)),
            pltpu.SemaphoreType.DMA((3, nlev)),
            pltpu.SemaphoreType.DMA((n_red,)),
            pltpu.SemaphoreType.DMA((n_red,)),
        ],
        compiler_params=pltpu.CompilerParams(
            collective_id=0, has_side_effects=True, vmem_limit_bytes=60 * 1024 * 1024),
    )(dual, obs_dual, increment, trajectory, model_var, obs_var, diffusion, obs_weight)


def solution(mesh):
    in_specs = (
        P("win", None, None, "ty", "tx"),
        P("win", None, "ty", "tx"),
        P("win", None, None, "ty", "tx"),
        P("win", None, None, None, "ty", "tx"),
        P(),
        P(),
        P("win", None, None, "ty", "tx"),
        P("win", None, "ty", "tx"),
    )
    out_specs = (
        P("win", None, None, "ty", "tx"),
        P("win", None, "ty", "tx"),
        P("win", None, None, "ty", "tx"),
        P(),
    )
    return jax.shard_map(
        functools.partial(per_device, mesh), mesh=mesh, in_specs=in_specs, out_specs=out_specs, check_vma=False
    )
```

```python
import functools
import jax
import jax.numpy as jnp
from jax import lax
from jax.experimental import pallas as pl
from jax.experimental.pallas import tpu as pltpu
from jax.sharding import PartitionSpec as P

MESH = pl.DeviceIdType.MESH
PAD = 8
EAST, WEST, NORTH, SOUTH = range(4)


def kernel(sizes, h_dual, h_obs, h_inc, h_traj, h_mv, h_ov, h_diff, h_wgt,
           o_lam, o_obs, o_inc, o_co,
           dual, obs, inc, traj, mv, ov, diff, wgt, i_sem,
           fld, grd, back, foll, plin, pls, pxs, gin, gout, oend, sbuf, rbuf, red,
           wsum, h_send, h_recv, w_send, w_recv, r_send, r_recv):
    nwin, ntx, nty, steps, nf, nlev, rows, nobs, count = sizes
    groups = rows // 8
    win, tx, ty = lax.axis_index("win"), lax.axis_index("tx"), lax.axis_index("ty")
    has_prev, has_next = win > 0, win < nwin - 1
    right, left = lax.rem(tx + 1, ntx), lax.rem(tx + ntx - 1, ntx)
    lane = lax.broadcasted_iota(jnp.int32, (8, 128), 1)
    is_last = (win == nwin - 1) & has_prev
    rounds = (
        (tx, ntx, [{"tx": lax.rem(tx + j, ntx)} for j in range(1, ntx)]),
        (ty * nwin + win, nty * nwin, [
            {"ty": lax.rem(ty + j // nwin, nty), "win": lax.rem(win + j % nwin, nwin)}
            for j in range(1, nty * nwin)]),
    )

    brought = [
        pltpu.make_async_copy(src, dst, i_sem.at[i])
        for i, (src, dst) in enumerate((
            (h_inc, inc), (h_diff, diff), (h_traj, traj), (h_obs, obs),
            (h_wgt, wgt), (h_dual, dual), (h_mv, mv), (h_ov, ov)))
    ]
    for copy in brought:
        copy.start()

    barrier = pltpu.get_barrier_semaphore()
    for _, _, partners in rounds:
        for partner in partners:
            pl.semaphore_signal(barrier, inc=1, device_id=partner, device_id_type=MESH)

    @pl.when(win == nwin - 1)
    def _():
        foll[...] = jnp.zeros(foll.shape, jnp.float32)
        plin[...] = jnp.zeros(plin.shape, jnp.float32)

    pl.semaphore_wait(barrier, (ntx - 1) + (nty * nwin - 1))

    north_of, south_of = lax.rem(ty + 1, nty), lax.rem(ty + nty - 1, nty)
    to = ({"tx": left}, {"tx": right}, {"ty": south_of}, {"ty": north_of})

    def start_halo(kind, s, c):
        for side in range(4):
            pltpu.make_async_remote_copy(
                src_ref=sbuf.at[kind, s, c, side], dst_ref=rbuf.at[kind, s, c, side],
                send_sem=h_send.at[kind], recv_sem=h_recv.at[kind, s, c],
                device_id=to[side], device_id_type=MESH).start()

    def wait_halo(kind, s, c):
        pltpu.make_async_remote_copy(
            src_ref=sbuf.at[kind, s, c], dst_ref=rbuf.at[kind, s, c],
            send_sem=h_send.at[kind], recv_sem=h_recv.at[kind, s, c],
            device_id=to[0], device_id_type=MESH).wait_recv()

    def edge_rows(kind, s, c):
        north = jnp.where(ty == nty - 1, 0.0, rbuf[kind, s, c, NORTH])
        south = jnp.where(ty == 0, 0.0, rbuf[kind, s, c, SOUTH])
        return north, south

    def wcopy(what, c):
        src, dst, to = (
            (h_dual.at[0, :, c], foll.at[c], win - 1),
            (pls.at[c], plin.at[c], win - 1),
            (gout.at[c], gin.at[c], win + 1),
        )[what]
        return pltpu.make_async_remote_copy(
            src_ref=src, dst_ref=dst, send_sem=w_send.at[what, c], recv_sem=w_recv.at[what, c],
            device_id={"win": to}, device_id_type=MESH)

    @pl.when(has_prev)
    def _():
        for c in range(2):
            wcopy(0, c).start()

    def loop(n, body):
        def step(i, carry):
            body(i)
            return carry
        lax.fori_loop(0, n, step, 0)

    def span(g):
        return pl.ds(8 * g, 8)

    def winds(s, c, g):
        a, b = traj[0, s, 0, c, span(g), :], traj[0, s, 1, c, span(g), :]
        pa, pb = jnp.maximum(a, 0.0), jnp.maximum(b, 0.0)
        ma, mb = pa - a, pb - b
        return pa, ma, pb, mb, 1.0 - ((pa + ma) + (pb + mb))

    pair = lane >> 1

    def into(acc, value, k):
        return jnp.where(pair == k, pltpu.roll(value, 2 * k + 1, 1), acc)

    def edge_columns(kind, s, c):
        return jnp.where(
            lane == 2 * pair, pltpu.roll(rbuf[kind, s, c, EAST], 127, 1), pltpu.roll(rbuf[kind, s, c, WEST], 1, 1))

    def shifted(for_east, for_west, columns, k):
        edge = pltpu.roll(columns, (127 - 2 * k) % 128, 1)
        east = jnp.where(lane == 127, edge, pltpu.roll(for_east, 127, 1))
        west = jnp.where(lane == 0, edge, pltpu.roll(for_west, 1, 1))
        return east, west

    zero_tile = jnp.zeros((8, 128), jnp.float32)

    def forward_first(c):
        packed = zero_tile
        for p in range(nf):
            for g in range(groups):
                value = inc[0, p, c, span(g), :]
                fld[0, c, p, pl.ds(PAD + 8 * g, 8), :] = value
                packed = into(packed, value, p * groups + g)
            sbuf[0, 0, c, NORTH, p, :] = inc[0, p, c, 0, :]
            sbuf[0, 0, c, SOUTH, p, :] = inc[0, p, c, rows - 1, :]
        sbuf[0, 0, c, EAST] = packed
        sbuf[0, 0, c, WEST] = packed
        start_halo(0, 0, c)


    def forward(s, c):
        wait_halo(0, s, c)
        now, later = lax.rem(s, 2), lax.rem(s + 1, 2)
        north_row, south_row = edge_rows(0, s, c)
        for p in range(nf):
            fld[now, c, p, PAD - 1, :] = south_row[p]
            fld[now, c, p, PAD + rows, :] = north_row[p]
        columns = edge_columns(0, s, c)
        packed = zero_tile
        ks = [diff[p, c] for p in range(nf)]
        after = jnp.minimum(s + 1, steps - 1)
        fresh = []
        for g in range(groups):
            pa, ma, pb, mb, d = winds(s, c, g)
            for p in range(nf):
                k = ks[p]
                x = fld[now, c, p, pl.ds(PAD + 8 * g, 8), :]
                north = fld[now, c, p, pl.ds(PAD + 8 * g + 1, 8), :]
                south = fld[now, c, p, pl.ds(PAD + 8 * g - 1, 8), :]
                place = p * groups + g
                east, west = shifted(x, x, columns, place)
                new = (d - 4.0 * k) * x + (pa + k) * west + (ma + k) * east + (pb + k) * south + (mb + k) * north
                fresh.append((p, g, new))
                packed = into(packed, new, place)
        for p, g, new in fresh:
            fld[later, c, p, pl.ds(PAD + 8 * g, 8), :] = new

        @pl.when(s < steps - 1)
        def _():
            for p in range(nf):
                sbuf[0, after, c, NORTH, p, :] = fld[later, c, p, PAD, :]
                sbuf[0, after, c, SOUTH, p, :] = fld[later, c, p, PAD + rows - 1, :]
            sbuf[0, after, c, EAST] = packed
            sbuf[0, after, c, WEST] = packed
            start_halo(0, after, c)

    moved = fld.at[steps % 2]

    def products(y, w, k, slot, c, p, g):
        pa, ma, pb, mb, d = w
        g_east, g_west = (pa + k) * y, (ma + k) * y
        here = pl.ds(PAD + 8 * g, 8)
        grd[slot, 0, c, p, here, :] = g_east
        grd[slot, 1, c, p, here, :] = g_west
        grd[slot, 2, c, p, here, :] = (pb + k) * y
        grd[slot, 3, c, p, here, :] = (mb + k) * y
        grd[slot, 4, c, p, here, :] = (d - 4.0 * k) * y
        return jnp.where(lane == 0, g_east, g_west)

    def ship(t, slot, c, packed):
        for p in range(nf):
            sbuf[1, t, c, NORTH, p, :] = grd[slot, 2, c, p, PAD, :]
            sbuf[1, t, c, SOUTH, p, :] = grd[slot, 3, c, p, PAD + rows - 1, :]
        sbuf[1, t, c, EAST] = packed
        sbuf[1, t, c, WEST] = packed
        start_halo(1, t, c)

    def adjoint_first(c):
        @pl.when(has_next)
        def _():
            wcopy(0, c).wait_recv()

        packed = zero_tile
        ks = [diff[p, c] for p in range(nf)]
        ws = [[wgt[o, p, c] for o in range(nobs)] for p in range(nf)]
        start = {}
        for g in range(groups):
            observed = [obs[0, o, span(g), :] for o in range(nobs)]
            for p in range(nf):
                y = -foll[c, p, span(g), :]
                for o in range(nobs):
                    y = y + ws[p][o] * observed[o]
                start[p, g] = y
        for g in range(groups):
            w = winds(steps - 1, c, g)
            for p in range(nf):
                packed = into(packed, products(start[p, g], w, ks[p], 0, c, p, g), p * groups + g)
        ship(0, 0, c, packed)


    def gathered(slot, c, p, g, columns):
        here = pl.ds(PAD + 8 * g, 8)
        east, west = shifted(grd[slot, 0, c, p, here, :], grd[slot, 1, c, p, here, :], columns, p * groups + g)
        north = grd[slot, 2, c, p, pl.ds(PAD + 8 * g + 1, 8), :]
        south = grd[slot, 3, c, p, pl.ds(PAD + 8 * g - 1, 8), :]
        return grd[slot, 4, c, p, here, :] + ((east + west) + (north + south))

    def receive(t, slot, c):
        wait_halo(1, t, c)
        north_row, south_row = edge_rows(1, t, c)
        for p in range(nf):
            grd[slot, 2, c, p, PAD + rows, :] = north_row[p]
            grd[slot, 3, c, p, PAD - 1, :] = south_row[p]
        return edge_columns(1, t, c)

    def adjoint(t, c):
        slot, other = lax.rem(t, 2), lax.rem(t + 1, 2)
        columns = receive(t, slot, c)
        packed = zero_tile
        ks = [diff[p, c] for p in range(nf)]
        start = {
            (p, g): gathered(slot, c, p, g, columns)
            for g in range(groups) for p in range(nf)}
        for g in range(groups):
            w = winds(steps - 2 - t, c, g)
            for p in range(nf):
                packed = into(packed, products(start[p, g], w, ks[p], other, c, p, g), p * groups + g)
        ship(t + 1, other, c, packed)


    def adjoint_last(c):
        slot = (steps - 1) % 2
        columns = receive(steps - 1, slot, c)
        done = {
            (p, g): gathered(slot, c, p, g, columns)
            for g in range(groups) for p in range(nf)}
        for (p, g), y in done.items():
            back[c, p, span(g), :] = y
        pls[c] = dual[0, :, c] + back[c]

        @pl.when(is_last)
        def _():
            wcopy(1, c).start()

    def fold(x):
        return jnp.sum(x.reshape(-1, 8, 128), axis=0)

    def suffix(c):
        @pl.when(has_next)
        def _():
            wcopy(1, c).wait_recv()
            pls[c] = pls[c] + plin[c]

        @pl.when(has_next & has_prev)
        def _():
            wcopy(1, c).start()

        lam = dual[0, :, c]
        new = pls[c]
        base = mv[0, :, c] * (lam - new) + inc[0, :, c]
        pxs[c] = base

        @pl.when((win == 0) & has_next)
        def _():
            gout[c] = base - moved[c, :, pl.ds(PAD, rows), :]
            wcopy(2, c).start()

        wsum[...] = wsum[...] + fold(new * lam)

    def follow(c):
        @pl.when(has_prev)
        def _():
            wcopy(0, c).wait_send()
            wcopy(0, c + 2).start()

    def slot_of_work(q):
        @pl.when((q >= 1) & (q <= steps))
        def _():
            loop(nlev, lambda c: forward(q - 1, c))

        for t in range(steps, -1, -1):
            @pl.when((q >= t) & (q - t < nlev))
            def _(t=t):
                if t == 0:
                    adjoint_first(q)
                elif t < steps:
                    adjoint(t - 1, q - t)
                else:
                    adjoint_last(q - t)

        @pl.when(q > steps)
        def _():
            suffix(q - steps - 1)

        for i in range(nlev - 2):
            pl.when(q == i)(lambda i=i: follow(i))

    brought[0].wait()
    loop(nlev, forward_first)
    for copy in brought[1:]:
        copy.wait()
    wsum[...] = zero_tile

    loop(nlev + steps + 1, slot_of_work)

    def observe(c, carry):
        return tuple(
            sum((wgt[o, p, c] * moved[c, p, pl.ds(PAD, rows), :] for p in range(nf)), carry[o])
            for o in range(nobs))

    ends = lax.fori_loop(0, nlev, observe, tuple(jnp.zeros((rows, 128), jnp.float32) for _ in range(nobs)))
    wv0, vv0 = wsum[...], zero_tile
    for o in range(nobs):
        v = obs[0, o]
        pm = (ov[0, o] * v + ends[o]) / ov[0, o]
        oend[o] = pm
        wv0 = wv0 + fold(pm * v)
        vv0 = vv0 + fold(v * v)

    def squares(c, acc):
        return acc + fold(dual[0, :, c] * dual[0, :, c]) + fold(inc[0, :, c] * inc[0, :, c])

    vv = lax.fori_loop(0, nlev, squares, vv0)

    def prefix(c, acc):
        @pl.when(has_prev)
        def _():
            wcopy(2, c).wait_recv()
            pxs[c] = pxs[c] + gin[c]

        @pl.when(has_prev & has_next)
        def _():
            gout[c] = pxs[c] - moved[c, :, pl.ds(PAD, rows), :]
            wcopy(2, c).start()

        return acc + fold(pxs[c] * inc[0, :, c])

    wv = lax.fori_loop(0, nlev, prefix, wv0)

    def total(x):
        return jnp.broadcast_to(jnp.sum(jnp.sum(x, axis=0, keepdims=True), axis=1, keepdims=True), (1, 128))

    def ratio(a, b):
        return jnp.where(b > 0.0, a / jnp.where(b > 0.0, b, 1.0), 0.0)

    wv, vv = total(wv), total(vv)
    h = ratio(wv, vv)

    def residual(c, acc):
        a = pls[c] - h[None] * dual[0, :, c]
        b = pxs[c] - h[None] * inc[0, :, c]
        return acc + fold(a * a) + fold(b * b)

    uu = zero_tile
    for o in range(nobs):
        r = oend[o] - h * obs[0, o]
        uu = uu + fold(r * r)
    uu = total(lax.fori_loop(0, nlev, residual, uu))

    at = 0
    for me, n, partners in rounds:
        red[at + me, 0:1, :] = uu
        red[at + me, 1:2, :] = wv
        red[at + me, 2:3, :] = vv
        swaps = [
            pltpu.make_async_remote_copy(
                src_ref=red.at[at + me], dst_ref=red.at[at + me],
                send_sem=r_send.at[at + j], recv_sem=r_recv.at[at + j],
                device_id=partner, device_id_type=MESH)
            for j, partner in enumerate(partners)]
        for swap in swaps:
            swap.start()
        for swap in swaps:
            swap.wait_recv()
        parts = [tuple(red[at + i, q:q + 1, :] for q in range(3)) for i in range(n)]
        wv = functools.reduce(lambda a, b: a + b, [q[1] for q in parts])
        vv = functools.reduce(lambda a, b: a + b, [q[2] for q in parts])
        h = ratio(wv, vv)
        uu = functools.reduce(
            lambda a, b: a + b, [q[0] + (ratio(q[1], q[2]) - h) * (ratio(q[1], q[2]) - h) * q[2] for q in parts])
        for swap in swaps:
            swap.wait_send()
        at += n

    h = wv / vv
    scale = jnp.sqrt(uu / count + 1e-06)
    inv = 1.0 / scale
    o_co[0] = jnp.sum(jnp.where(lane[0:1] == 0, h, 0.0))
    o_co[1] = jnp.sum(jnp.where(lane[0:1] == 0, scale, 0.0))

    def finish(c):
        o_lam[0, :, c] = (pls[c] - h[None] * dual[0, :, c]) * inv[None]
        o_inc[0, :, c] = (pxs[c] - h[None] * inc[0, :, c]) * inv[None]

    loop(nlev, finish)
    for o in range(nobs):
        o_obs[0, o] = (oend[o] - h * obs[0, o]) * inv

    for kind in range(2):
        pltpu.make_async_remote_copy(
            src_ref=sbuf.at[kind], dst_ref=rbuf.at[kind], send_sem=h_send.at[kind],
            recv_sem=h_recv.at[kind, 0, 0], device_id=to[0], device_id_type=MESH).wait_send()

    def settle(c):
        @pl.when(has_prev)
        def _():
            wcopy(1, c).wait_send()

        @pl.when(has_prev & (c >= nlev - 2))
        def _():
            wcopy(0, c).wait_send()

        @pl.when(has_next)
        def _():
            wcopy(2, c).wait_send()

    loop(nlev, settle)


def per_device(mesh, dual, obs_dual, increment, trajectory, diffusion, obs_weight, model_var, obs_var):
    nwin, ntx, nty = (mesh.shape[a] for a in ("win", "tx", "ty"))
    _, nf, nlev, rows, cols = dual.shape
    nobs, steps = obs_dual.shape[1], trajectory.shape[1]
    assert cols == 128 and rows % 8 == 0 and nlev >= 2 and nf * rows // 4 <= 128 and nf <= 8
    count = (2 * nf * nlev + nobs) * rows * cols * nwin * ntx * nty
    sizes = (nwin, ntx, nty, steps, nf, nlev, rows, nobs, float(count))
    vmem, smem = pl.BlockSpec(memory_space=pltpu.VMEM), pl.BlockSpec(memory_space=pltpu.SMEM)
    chunks = pltpu.VMEM((nlev, nf, rows, cols), jnp.float32)
    messages = pltpu.VMEM((2, steps, nlev, 4, 8, cols), jnp.float32)
    n_red = ntx + nty * nwin
    return pl.pallas_call(
        functools.partial(kernel, sizes),
        out_shape=(
            jax.ShapeDtypeStruct(dual.shape, jnp.float32),
            jax.ShapeDtypeStruct(obs_dual.shape, jnp.float32),
            jax.ShapeDtypeStruct(increment.shape, jnp.float32),
            jax.ShapeDtypeStruct((2,), jnp.float32),
        ),
        in_specs=[pl.BlockSpec(memory_space=pltpu.HBM)] * 8,
        out_specs=(vmem, vmem, vmem, smem),
        scratch_shapes=[
            pltpu.VMEM(dual.shape, jnp.float32), pltpu.VMEM(obs_dual.shape, jnp.float32),
            pltpu.VMEM(increment.shape, jnp.float32), pltpu.VMEM(trajectory.shape, jnp.float32),
            pltpu.VMEM(model_var.shape, jnp.float32), pltpu.VMEM(obs_var.shape, jnp.float32),
            pltpu.SMEM(diffusion.shape, jnp.float32), pltpu.SMEM(obs_weight.shape, jnp.float32),
            pltpu.SemaphoreType.DMA((8,)),
            pltpu.VMEM((2, nlev, nf, rows + 2 * PAD, cols), jnp.float32),
            pltpu.VMEM((2, 5, nlev, nf, rows + 2 * PAD, cols), jnp.float32),
            chunks, chunks, chunks, chunks, chunks, chunks, chunks,
            pltpu.VMEM((nobs, rows, cols), jnp.float32),
            messages, messages,
            pltpu.VMEM((n_red, 8, cols), jnp.float32),
            pltpu.VMEM((8, cols), jnp.float32),
            pltpu.SemaphoreType.DMA((2,)),
            pltpu.SemaphoreType.DMA((2, steps, nlev)),
            pltpu.SemaphoreType.DMA((3, nlev)),
            pltpu.SemaphoreType.DMA((3, nlev)),
            pltpu.SemaphoreType.DMA((n_red,)),
            pltpu.SemaphoreType.DMA((n_red,)),
        ],
        compiler_params=pltpu.CompilerParams(
            collective_id=0, has_side_effects=True, vmem_limit_bytes=60 * 1024 * 1024),
    )(dual, obs_dual, increment, trajectory, model_var, obs_var, diffusion, obs_weight)


def solution(mesh):
    in_specs = (
        P("win", None, None, "ty", "tx"),
        P("win", None, "ty", "tx"),
        P("win", None, None, "ty", "tx"),
        P("win", None, None, None, "ty", "tx"),
        P(),
        P(),
        P("win", None, None, "ty", "tx"),
        P("win", None, "ty", "tx"),
    )
    out_specs = (
        P("win", None, None, "ty", "tx"),
        P("win", None, "ty", "tx"),
        P("win", None, None, "ty", "tx"),
        P(),
    )
    return jax.shard_map(
        functools.partial(per_device, mesh), mesh=mesh, in_specs=in_specs, out_specs=out_specs, check_vma=False
    )
```
